256 devices in a mesh: outer: 16 (over y_hi, z), inner: 16 (over x, y_lo, core).
Axes of the slice: x: 4, y: 4 (y_hi: 2, y_lo: 2; y = y_hi * 2 + y_lo), z: 8, core: 2. Of those that a mesh axis runs over, the one named last changes fastest.
Arguments:
- queries: bfloat16 [98304, 1024], P(('outer', 'inner')), may hold values from -80 to 80
- keys: bfloat16 [98304, 128], P(('outer', 'inner')), may hold values from -6 to 6
- values: bfloat16 [98304, 128], P(('outer', 'inner')), may hold values from -6 to 6
- saved_out: bfloat16 [98304, 1024], P(('outer', 'inner')), may hold values from -6 to 6
- saved_lse: float32 [98304, 8], P(('outer', 'inner')), may hold values from -20 to 250, as said below
- out_grad: bfloat16 [98304, 1024], P(('outer', 'inner')), may hold values from -24 to 24
- positions: int32 [98304], P(('outer', 'inner')), may hold values from 0 to 98303, as said below
Outputs:
- query_grad: bfloat16 [98304, 1024], P(('outer', 'inner'))
- key_grad: bfloat16 [98304, 128], P(('outer', 'inner'))
- value_grad: bfloat16 [98304, 128], P(('outer', 'inner'))
The draws below stay inside these ranges and needn't reach their ends.
Inputs may be any that keep to these rules, and one draw needn't show every extreme that they name: saved_lse[t, h] is the log of the sum over the allowed u of exp(scores[h, t, u]), computed in float32. positions is a permutation of the token positions; the rows of each block are two runs of 192 consecutive ascending positions, the first starting at c * 192 and the second at (511 - c) * 192, where c differs from block to block.
All inputs are finite; a program needn't handle non-finite values.
Results may differ from the reference program's by a relative error of at most 0.006.
Values may be sent and summed in bfloat16 or wider, within the bound.
A program may use at most 128 MiB of HBM per device.

```python
import jax
import jax.numpy as jnp
from jax import lax

HD = 128
H = 8
TOK_DEV = 384
SPAN = 192
TOKENS = 98304
INNER_STEPS = 4
N_OUTER = 16
N_INNER = 16


def draw_keys(key, part):
    key = jax.random.fold_in(key, 5)
    result = jnp.clip(jax.random.normal(key, (TOKENS, HD), jnp.float32), -6.0, 6.0)
    return result.astype(jnp.bfloat16)


def draw_queries(key, part):
    key = jax.random.fold_in(key, 7)
    result = jax.random.normal(key, (TOKENS, H * HD), jnp.float32)
    return result.astype(jnp.bfloat16)


def draw_positions(key, part):
    key = jax.random.fold_in(key, 3)
    block_total = N_OUTER * N_INNER
    order = jax.random.permutation(key, block_total).astype(jnp.int32)
    offsets = jnp.arange(SPAN, dtype=jnp.int32)
    first = order[:, None] * SPAN + offsets[None, :]
    second = (2 * block_total - 1 - order)[:, None] * SPAN + offsets[None, :]
    return jnp.concatenate([first, second], axis=1).reshape(TOKENS).astype(jnp.int32)


def draw_saved_lse(key, part):
    query3 = draw_queries(key, part).astype(jnp.float32).reshape(TOKENS, H, HD)
    key_rows = draw_keys(key, part).astype(jnp.float32)
    pos = draw_positions(key, part)

    def take(array, block):
        return lax.dynamic_slice_in_dim(array, (block * TOK_DEV).astype(jnp.int32), TOK_DEV, 0)

    def one_block(block):
        group = block // N_INNER
        place = block % N_INNER
        owners = [block]
        for step in range(1, INNER_STEPS + 1):
            owners.append(group * N_INNER + (place - step) % N_INNER)
        owners.append((group - 1) % N_OUTER * N_INNER + place)
        key_all = jnp.concatenate([take(key_rows, j) for j in owners], axis=0)
        key_pos = jnp.concatenate([take(pos, j) for j in owners], axis=0)
        scores = jnp.einsum('thd,ud->thu', take(query3, block), key_all, precision=lax.Precision.HIGHEST) * HD ** (-0.5)
        allowed = key_pos[None, None, :] <= take(pos, block)[:, None, None]
        scores = jnp.where(allowed, scores, -jnp.inf)
        top = jnp.max(scores, axis=-1)
        return top + jnp.log(jnp.sum(jnp.exp(scores - top[:, :, None]), axis=-1))
    result = lax.map(one_block, jnp.arange(N_OUTER * N_INNER, dtype=jnp.int32))
    return result.reshape(TOKENS, H).astype(jnp.float32)


def level_of(stream_key, shape, cuts, smallest, largest):
    factor_of, own = 1.0, jax.random.fold_in(stream_key, 6)
    for axis_at, shards_of in cuts:
        steps = jnp.exp(jax.random.uniform(jax.random.fold_in(own, axis_at), (shards_of,), jnp.float32, smallest / len(cuts), largest / len(cuts)))
        factor_of = factor_of * jnp.repeat(steps, shape[axis_at] // shards_of).reshape([-1 if axis == axis_at else 1 for axis in range(len(shape))])
    return factor_of


def centred(stream_key, shape, deviation, most, cuts=(), kind=jnp.bfloat16):
    level = level_of(stream_key, shape, cuts, -0.22, 0.18) if cuts else 1.0
    drawn = jax.random.normal(stream_key, shape, jnp.float32) * deviation * level
    return jnp.minimum(jnp.maximum(drawn, -most), most).astype(kind)


def setup_inputs(seed: int = 0) -> dict:
    splits = jax.random.split(jax.random.key(seed), 8)
    queries = draw_queries(jax.random.fold_in(splits[7], 71), 0)
    keys = draw_keys(jax.random.fold_in(splits[7], 71), 0)
    values = centred(splits[2], (TOKENS, HD), 1.0, 6.0, ((0, 256),))
    saved_out = centred(splits[3], (TOKENS, H * HD), 1.0, 6.0, ((0, 256),))
    saved_lse = draw_saved_lse(jax.random.fold_in(splits[7], 71), 0)
    out_grad = centred(splits[5], (TOKENS, H * HD), 4.0, 24.0, ((0, 256),))
    positions = draw_positions(jax.random.fold_in(splits[7], 71), 0)
    return dict(queries=queries, keys=keys, values=values, saved_out=saved_out, saved_lse=saved_lse, out_grad=out_grad, positions=positions)


def block_terms(query_part, key_all, value_all, saved_part, grad_part, lse_part, query_pos, key_pos):
    score_scale = HD ** -0.5
    scores = jnp.einsum('thd,ud->htu', query_part.astype(jnp.float32), key_all.astype(jnp.float32)) * score_scale
    allowed = key_pos[None, None, :] <= query_pos[None, :, None]
    probs = jnp.where(allowed, jnp.exp(jnp.where(allowed, scores, 0.0) - lse_part.T[:, :, None]), 0.0)
    probs_b = probs.astype(jnp.bfloat16)
    value_term = jnp.einsum('htu,thd->ud', probs_b.astype(jnp.float32), grad_part.astype(jnp.float32))
    dprobs = jnp.einsum('thd,ud->htu', grad_part.astype(jnp.float32), value_all.astype(jnp.float32))
    row_dots = jnp.sum(grad_part.astype(jnp.float32) * saved_part.astype(jnp.float32), axis=-1).T
    dscores = (probs * (dprobs - row_dots[:, :, None])).astype(jnp.bfloat16)
    query_term = jnp.einsum('htu,ud->thd', dscores.astype(jnp.float32), key_all.astype(jnp.float32)) * score_scale
    key_term = jnp.einsum('htu,thd->ud', dscores.astype(jnp.float32), query_part.astype(jnp.float32)) * score_scale
    return query_term, key_term, value_term


def reference(queries, keys, values, saved_out, saved_lse, out_grad, positions):
    query3 = queries.reshape(TOKENS, H, HD)
    saved3 = saved_out.reshape(TOKENS, H, HD)
    grad3 = out_grad.reshape(TOKENS, H, HD)

    def take(array, block):
        return lax.dynamic_slice_in_dim(array, (block * TOK_DEV).astype(jnp.int32), TOK_DEV, 0)

    def one_block(carry, block):
        key_acc, value_acc = carry
        group = block // N_INNER
        place = block % N_INNER
        owners = [block]
        for step in range(1, INNER_STEPS + 1):
            owners.append(group * N_INNER + (place - step) % N_INNER)
        owners.append(((group - 1) % N_OUTER) * N_INNER + place)
        key_all = jnp.concatenate([take(keys, j) for j in owners], axis=0)
        value_all = jnp.concatenate([take(values, j) for j in owners], axis=0)
        key_pos = jnp.concatenate([take(positions, j) for j in owners], axis=0)
        query_term, key_term, value_term = block_terms(take(query3, block), key_all, value_all, take(saved3, block), take(grad3, block), take(saved_lse, block), take(positions, block), key_pos)
        for count, owner in enumerate(owners):
            start = (owner * TOK_DEV).astype(jnp.int32)
            key_acc = lax.dynamic_update_slice_in_dim(key_acc, take(key_acc, owner) + key_term[count * TOK_DEV:(count + 1) * TOK_DEV], start, 0)
            value_acc = lax.dynamic_update_slice_in_dim(value_acc, take(value_acc, owner) + value_term[count * TOK_DEV:(count + 1) * TOK_DEV], start, 0)
        return (key_acc, value_acc), query_term.reshape(TOK_DEV, H * HD).astype(jnp.bfloat16)

    zeros = jnp.zeros((TOKENS, HD), jnp.float32)
    (key_acc, value_acc), query_blocks = lax.scan(one_block, (zeros, zeros), jnp.arange(N_OUTER * N_INNER, dtype=jnp.int32))
    return query_blocks.reshape(TOKENS, H * HD), key_acc.astype(jnp.bfloat16), value_acc.astype(jnp.bfloat16)
```

```python
import functools

import jax
import jax.numpy as jnp
import numpy as np
from jax import lax
from jax.experimental import pallas as pl
from jax.experimental.pallas import tpu as pltpu
from jax.sharding import PartitionSpec as P

F32 = jnp.float32
BF16 = jnp.bfloat16
REACH = 4
FAR = REACH + 1


def nn(a, b):
    return lax.dot_general(a, b, (((1,), (0,)), ((), ())), preferred_element_type=F32)


def nt(a, b):
    return lax.dot_general(a, b, (((1,), (1,)), ((), ())), preferred_element_type=F32)


def tn(a, b):
    return lax.dot_general(a, b, (((0,), (0,)), ((), ())), preferred_element_type=F32)


def kernel(
    n_outer,
    n_inner,
    q_hbm,
    k_hbm,
    v_hbm,
    o_hbm,
    lse_ref,
    g_hbm,
    pos_ref,
    dq_ref,
    dk_ref,
    dv_ref,
    qs,
    gs,
    yq,
    yg,
    o_vm,
    kv,
    mark,
    marks,
    dqt,
    own,
    terms,
    came,
    load_sem,
    kv_sem,
    mark_send,
    mark_recv,
    mark_load,
    put_sem,
    get_sem,
    term_send,
    term_recv,
):
    outer = lax.axis_index("outer")
    inner = lax.axis_index("inner")
    span, width = kv.shape[3], kv.shape[4]
    heads = q_hbm.shape[1] // width
    scale = width**-0.5
    exp_scale = float(np.log2(np.e)) * scale
    core = lax.rem(inner, 2)
    side = lax.rem(inner // 2, 2)

    def inner_at(step):
        return (outer, lax.rem(inner + n_inner + step, n_inner))

    def outer_at(step):
        return (lax.rem(outer + n_outer + step, n_outer), inner)

    loads = []
    for src, dst in ((k_hbm, 0), (v_hbm, 1)):
        for half in range(2):
            copy = pltpu.make_async_copy(
                src.at[pl.ds(half * span, span), :], kv.at[0, dst, half], kv_sem.at[dst, half]
            )
            copy.start()
            loads.append(copy)
    tiles = []
    for at, (src, dst) in enumerate(((g_hbm, gs), (q_hbm, qs))):
        for half in range(2):
            for h in range(heads):
                pltpu.make_async_copy(
                    src.at[pl.ds(half * span, span), pl.ds(h * width, width)],
                    dst.at[half, pl.ds(h * span, span), :],
                    load_sem.at[at],
                ).start()
    o_copy = pltpu.make_async_copy(o_hbm, o_vm, load_sem.at[2])
    o_copy.start()

    barrier = pltpu.get_barrier_semaphore()
    friends = [inner_at(s) for s in range(-REACH, REACH + 1) if s] + [outer_at(-1), outer_at(1)]
    for friend in friends:
        pl.semaphore_signal(barrier, inc=1, device_id=friend, device_id_type=pl.DeviceIdType.MESH)
    first = pos_ref[0] // span
    mark[...] = jnp.full(mark.shape, first, jnp.int32)
    for copy in loads:
        copy.wait()
    pl.semaphore_wait(barrier, len(friends))

    def put(src_slot, slot, target):
        return pltpu.make_async_remote_copy(
            src_ref=kv.at[src_slot],
            dst_ref=kv.at[slot],
            send_sem=put_sem.at[slot],
            recv_sem=get_sem.at[slot],
            device_id=target,
            device_id_type=pl.DeviceIdType.MESH,
        )

    core_mate = (outer, inner + 1 - 2 * core)
    side_mate = (outer, inner + 2 - 4 * side)
    put4 = put(0, 4, inner_at(4))
    put5 = put(0, FAR, outer_at(1))
    put2 = put(4 * side, 2, side_mate)
    put1 = put(2 * core, 1, core_mate)
    put3 = put(2 + 2 * core, 3, core_mate)
    put4.start()
    put5.start()

    @pl.when(side == 0)
    def _():
        put2.start()

    @pl.when(core == 0)
    def _():
        put1.start()

    mark_puts = []
    for slot in range(1, FAR + 1):
        copy = pltpu.make_async_remote_copy(
            src_ref=mark,
            dst_ref=marks.at[slot],
            send_sem=mark_send.at[slot],
            recv_sem=mark_recv.at[slot],
            device_id=outer_at(1) if slot == FAR else inner_at(slot),
            device_id_type=pl.DeviceIdType.MESH,
        )
        copy.start()
        mark_puts.append(copy)

    pltpu.make_async_copy(gs, gs, load_sem.at[0]).wait()
    o_copy.wait()
    lane = lax.broadcasted_iota(jnp.int32, (span, width), 1)
    spread = jnp.where(lane < 3 * heads, lax.rem(lane, heads), -1)

    def split(x):
        hi = x.astype(BF16).astype(F32)
        mid = (x - hi).astype(BF16).astype(F32)
        return jnp.where(lane < heads, hi, jnp.where(lane < 2 * heads, mid, x - hi - mid))

    norm_rows = jnp.concatenate(
        [lse_ref[...] * (1.0 / scale)] * 3 + [jnp.zeros((width - 3 * heads, 2 * span), F32)], 0
    )
    norm_table = norm_rows.T
    for half in range(2):
        rows = pl.ds(half * span, span)
        dots = jnp.zeros((span, width), F32)
        for h in range(heads):
            g = gs[half, pl.ds(h * span, span), :].astype(F32)
            o = o_vm[rows, pl.ds(h * width, width)].astype(F32)
            dots = jnp.where(spread == h, jnp.sum(g * o, axis=1, keepdims=True), dots)
        dots, norms = split(dots), split(norm_table[half * span : (half + 1) * span])
        for h in range(heads):
            to = pl.ds(h * span, span)
            yg[half, to, :] = jnp.where(spread == h, dots, 0.0).astype(BF16)
            yq[half, to, :] = jnp.where(spread == h, norms, 0.0).astype(BF16)
    minus = jnp.where(lane < 3 * heads, -1.0, 0.0).astype(BF16)

    columns = heads * span
    high = jnp.where(first < n_outer * n_inner, 1, 0)
    low = 1 - high

    def unit(slot, key_half, query_half, diagonal):
        k, v = (lax.select(key_half == 1, kv[slot, at, 1], kv[slot, at, 0]) for at in range(2))
        q, g = qs[query_half], gs[query_half]
        scores = nt(jnp.concatenate([k, minus], 1), jnp.concatenate([q, yq[query_half]], 1))
        probs = jnp.exp2(scores * exp_scale)
        if diagonal:
            t = lax.rem(lax.broadcasted_iota(jnp.int32, (1, columns), 1), span)
            u = lax.broadcasted_iota(jnp.int32, (span, 1), 0)
            probs = jnp.where(u <= t, probs, 0.0)
        probs_b = probs.astype(BF16)
        shifted = nt(jnp.concatenate([v, minus], 1), jnp.concatenate([g, yg[query_half]], 1))
        dscores = (probs * shifted).astype(BF16)
        return nn(dscores, q), nn(probs_b, g), tn(k, dscores)

    pltpu.make_async_copy(qs, qs, load_sem.at[1]).wait()

    dk, dv, dq = unit(0, low, low, True)
    own[0, 0], own[1, 0], dqt[0] = dk, dv, dq
    dk, dv, dq = unit(0, low, high, False)
    own[0, 0] += dk
    own[1, 0] += dv
    dqt[1] = dq
    dk, dv, dq = unit(0, high, high, True)
    own[0, 1], own[1, 1] = dk, dv
    dqt[1] += dq

    mark_loads = []
    for slot in range(1, FAR + 1):
        mark_puts[slot - 1].wait_recv()
        copy = pltpu.make_async_copy(marks.at[slot], mark_load.at[slot], mark_recv.at[slot])
        mark_loads.append(copy)
        copy.start()
    for copy in mark_loads:
        copy.wait()

    def term_put(slot):
        far = slot // FAR
        target = (
            lax.rem(outer + (n_outer - 1) * far, n_outer),
            lax.rem(inner + (n_inner - slot) * (1 - far), n_inner),
        )
        return pltpu.make_async_remote_copy(
            src_ref=terms.at[slot],
            dst_ref=came.at[slot],
            send_sem=term_send.at[slot],
            recv_sem=term_recv.at[slot],
            device_id=target,
            device_id_type=pl.DeviceIdType.MESH,
        )

    order = (4, FAR, 2, 1, 3)
    packed = sum(slot * 8**at for at, slot in enumerate(order))

    def step(_, rest):
        slot, rest = lax.rem(rest, 8), rest // 8
        put(0, slot, core_mate).wait_recv()

        @pl.when((slot == 4) & (side == 1))
        def _():
            put2.start()

        @pl.when(((slot == 4) & (core == 1)) | ((slot == 2) & (core == 0)))
        def _():
            put3.start()

        @pl.when((slot == 2) & (core == 1))
        def _():
            put1.start()

        there = mark_load[slot, 0, 0]
        there_low = jnp.where(there < n_outer * n_inner, 0, 1)
        run_here = jnp.minimum(first, 2 * n_outer * n_inner - 1 - first)
        run_there = jnp.minimum(there, 2 * n_outer * n_inner - 1 - there)
        earlier = run_there < run_here
        keep = jnp.where(earlier, 1.0, 0.0)
        dk, dv, dq = unit(slot, there_low, high, False)
        key_half = jnp.where(earlier, there_low, 1 - there_low)
        query_half = jnp.where(earlier, low, high)
        dk2, dv2, dq2 = unit(slot, key_half, query_half, False)
        dq_low = dq2 * keep
        dqt[0] += dq_low
        dqt[1] += dq + (dq2 - dq_low)
        for at, (one, two) in enumerate(((dk, dk2), (dv, dv2))):
            two_low = two * keep
            factor = 1.0 if at else scale
            terms[slot, at, 0] = ((one + two_low) * factor).astype(BF16)
            terms[slot, at, 1] = ((two - two_low) * factor).astype(BF16)
        term_put(slot).start()
        return rest

    lax.fori_loop(0, len(order), step, packed)

    for half in range(2):
        rank = jnp.where(first < n_outer * n_inner, half, 1 - half)
        dq = (dqt[rank] * scale).T.astype(BF16)
        for h in range(heads):
            dq_ref[pl.ds(half * span, span), pl.ds(h * width, width)] = dq[h * span : (h + 1) * span]

    for slot in range(1, FAR + 1):
        term_put(jnp.int32(slot)).wait_recv()
    for at, out in enumerate((dk_ref, dv_ref)):
        for half in range(2):
            rank = jnp.where(first < n_outer * n_inner, half, 1 - half)
            total = own[at, rank] * (1.0 if at else scale)
            for slot in range(1, FAR + 1):
                total += came[slot, at, rank].astype(F32)
            out[pl.ds(half * span, span), :] = total.astype(BF16)

    for copy in mark_puts:
        copy.wait_send()
    for copy in (put1, put2, put3, put4, put5):
        copy.wait_send()
    for slot in range(1, FAR + 1):
        term_put(jnp.int32(slot)).wait_send()


def shards(queries, keys, values, saved_out, saved_lse, out_grad, positions):
    rows, columns = queries.shape
    width = keys.shape[1]
    span = rows // 2
    heads = columns // width
    anywhere = pl.BlockSpec(memory_space=pl.ANY)
    vmem = pl.BlockSpec(memory_space=pltpu.VMEM)
    slots = FAR + 1
    stack = (2, heads * span, width)
    pair = (2, 2, span, width)
    dma = pltpu.SemaphoreType.DMA
    return pl.pallas_call(
        functools.partial(kernel, lax.axis_size("outer"), lax.axis_size("inner")),
        out_shape=(
            jax.ShapeDtypeStruct(queries.shape, BF16),
            jax.ShapeDtypeStruct(keys.shape, BF16),
            jax.ShapeDtypeStruct(values.shape, BF16),
        ),
        in_specs=[
            anywhere,
            anywhere,
            anywhere,
            anywhere,
            vmem,
            anywhere,
            pl.BlockSpec(memory_space=pltpu.SMEM),
        ],
        out_specs=[vmem] * 3,
        scratch_shapes=[
            pltpu.VMEM(stack, BF16),
            pltpu.VMEM(stack, BF16),
            pltpu.VMEM(stack, BF16),
            pltpu.VMEM(stack, BF16),
            pltpu.VMEM((rows, columns), BF16),
            pltpu.VMEM((slots,) + pair, BF16),
            pltpu.VMEM((8, 128), jnp.int32),
            pltpu.VMEM((slots, 8, 128), jnp.int32),
            pltpu.VMEM((2, width, heads * span), F32),
            pltpu.VMEM(pair, F32),
            pltpu.VMEM((slots,) + pair, BF16),
            pltpu.VMEM((slots,) + pair, BF16),
            dma((3,)),
            dma((2, 2)),
            dma((slots,)),
            dma((slots,)),
            pltpu.SMEM((slots, 8, 128), jnp.int32),
            dma((slots,)),
            dma((slots,)),
            dma((slots,)),
            dma((slots,)),
        ],
        compiler_params=pltpu.CompilerParams(
            collective_id=0, has_side_effects=True, vmem_limit_bytes=56 * 2**20
        ),
    )(queries, keys, values, saved_out, saved_lse.T, out_grad, positions)


def solution(mesh):
    rows = P(("outer", "inner"), None)
    return jax.shard_map(
        shards,
        mesh=mesh,
        in_specs=(rows,) * 6 + (P(("outer", "inner")),),
        out_specs=(rows,) * 3,
        check_vma=False,
    )
```

```python
import functools

import jax
import jax.numpy as jnp
import numpy as np
from jax import lax
from jax.experimental import pallas as pl
from jax.experimental.pallas import tpu as pltpu
from jax.sharding import PartitionSpec as P

F32 = jnp.float32
BF16 = jnp.bfloat16
REACH = 4
FAR = REACH + 1


def nn(a, b):
    return lax.dot_general(a, b, (((1,), (0,)), ((), ())), preferred_element_type=F32)


def nt(a, b):
    return lax.dot_general(a, b, (((1,), (1,)), ((), ())), preferred_element_type=F32)


def tn(a, b):
    return lax.dot_general(a, b, (((0,), (0,)), ((), ())), preferred_element_type=F32)


def kernel(
    n_outer,
    n_inner,
    q_hbm,
    k_hbm,
    v_hbm,
    o_hbm,
    lse_ref,
    g_hbm,
    pos_ref,
    dq_ref,
    dk_ref,
    dv_ref,
    qs,
    gs,
    yq,
    yg,
    o_vm,
    kv,
    mark,
    marks,
    dqt,
    own,
    terms,
    came,
    load_sem,
    kv_sem,
    mark_send,
    mark_recv,
    mark_load,
    put_sem,
    get_sem,
    term_send,
    term_recv,
    gate,
):
    outer = lax.axis_index("outer")
    inner = lax.axis_index("inner")
    span, width = kv.shape[3], kv.shape[4]
    heads = q_hbm.shape[1] // width
    scale = width**-0.5
    exp_scale = float(np.log2(np.e)) * scale
    core = lax.rem(inner, 2)

    def inner_at(step):
        return (outer, lax.rem(inner + n_inner + step, n_inner))

    def outer_at(step):
        return (lax.rem(outer + n_outer + step, n_outer), inner)

    loads = []
    for src, dst in ((k_hbm, 0), (v_hbm, 1)):
        for half in range(2):
            copy = pltpu.make_async_copy(
                src.at[pl.ds(half * span, span), :], kv.at[0, dst, half], kv_sem.at[dst, half]
            )
            copy.start()
            loads.append(copy)

    def remote(src, dst, send_sem, recv_sem, target):
        return pltpu.make_async_remote_copy(
            src_ref=src,
            dst_ref=dst,
            send_sem=send_sem,
            recv_sem=recv_sem,
            device_id=target,
            device_id_type=pl.DeviceIdType.MESH,
        )

    def signal(semaphore, target):
        pl.semaphore_signal(semaphore, 1, device_id=target, device_id_type=pl.DeviceIdType.MESH)

    barrier = pltpu.get_barrier_semaphore()
    mate = (outer, inner + 1 - 2 * core)

    @pl.when(core == 0)
    def _():
        for step in (-4, -2, 2, 4):
            signal(barrier, inner_at(step))
        for step in (-1, 1):
            signal(barrier, (outer_at(step)[0], inner + 1))

    @pl.when(core == 1)
    def _():
        for step in (-5, -3, -1, 1, 3):
            signal(barrier, inner_at(step))
        for step in (-1, 1):
            signal(barrier, outer_at(step))

    for at, (src, dst) in enumerate(((g_hbm, gs), (q_hbm, qs))):
        for half in range(2):
            for h in range(heads):
                pltpu.make_async_copy(
                    src.at[pl.ds(half * span, span), pl.ds(h * width, width)],
                    dst.at[half, pl.ds(h * span, span), :],
                    load_sem.at[at],
                ).start()
        if at == 0:
            o_copy = pltpu.make_async_copy(o_hbm, o_vm, load_sem.at[2])
            o_copy.start()
    first = pos_ref[0] // span
    mark[...] = jnp.full(mark.shape, first, jnp.int32)
    for copy in loads:
        copy.wait()

    @pl.when(core == 0)
    def _():
        pl.semaphore_wait(barrier, 9)
        signal(gate, mate)

    @pl.when(core == 1)
    def _():
        pl.semaphore_wait(gate, 1)

    def put(src_slot, slot, target):
        return remote(kv.at[src_slot], kv.at[slot], put_sem.at[slot], get_sem.at[slot], target)

    put5 = put(0, FAR, outer_at(1))
    put4 = put(0, 4, inner_at(4))
    put2 = put(0, 2, inner_at(2))
    put1 = put(2 * core, 1, mate)
    put3 = put(2 + 2 * core, 3, mate)
    mark_puts = [
        remote(
            mark,
            marks.at[slot],
            mark_send.at[slot],
            mark_recv.at[slot],
            outer_at(1) if slot == FAR else inner_at(slot),
        )
        for slot in range(1, FAR + 1)
    ]
    for copy in mark_puts[:REACH]:
        copy.start()

    @pl.when(core == 0)
    def _():
        put1.start()

    put4.start()
    put2.start()

    def reach_outer():
        @pl.when(core == 1)
        def _():
            pl.semaphore_wait(barrier, 4)
            signal(gate, mate)

        @pl.when(core == 0)
        def _():
            pl.semaphore_wait(gate, 1)

        mark_puts[REACH].start()
        put5.start()

    early = lax.rem(outer, 8) == 0

    @pl.when(jnp.logical_not(early))
    def _():
        reach_outer()

    pltpu.make_async_copy(gs, gs, load_sem.at[0]).wait()
    o_copy.wait()
    lane = lax.broadcasted_iota(jnp.int32, (span, width), 1)
    spread = jnp.where(lane < 3 * heads, lax.rem(lane, heads), -1)

    def split(x):
        hi = x.astype(BF16).astype(F32)
        mid = (x - hi).astype(BF16).astype(F32)
        return jnp.where(lane < heads, hi, jnp.where(lane < 2 * heads, mid, x - hi - mid))

    norm_rows = jnp.concatenate(
        [lse_ref[...] * (1.0 / scale)] * 3 + [jnp.zeros((width - 3 * heads, 2 * span), F32)], 0
    )
    norm_table = norm_rows.T
    for half in range(2):
        rows = pl.ds(half * span, span)
        dots = jnp.zeros((span, width), F32)
        for h in range(heads):
            g = gs[half, pl.ds(h * span, span), :].astype(F32)
            o = o_vm[rows, pl.ds(h * width, width)].astype(F32)
            dots = jnp.where(spread == h, jnp.sum(g * o, axis=1, keepdims=True), dots)
        dots, norms = split(dots), split(norm_table[half * span : (half + 1) * span])
        for h in range(heads):
            to = pl.ds(h * span, span)
            yg[half, to, :] = jnp.where(spread == h, dots, 0.0).astype(BF16)
            yq[half, to, :] = jnp.where(spread == h, norms, 0.0).astype(BF16)
    minus = jnp.where(lane < 3 * heads, -1.0, 0.0).astype(BF16)

    columns = heads * span
    high = jnp.where(first < n_outer * n_inner, 1, 0)
    low = 1 - high

    def unit(slot, key_half, query_half, diagonal):
        k, v = (lax.select(key_half == 1, kv[slot, at, 1], kv[slot, at, 0]) for at in range(2))
        q, g = qs[query_half], gs[query_half]
        scores = nt(jnp.concatenate([k, minus], 1), jnp.concatenate([q, yq[query_half]], 1))
        probs = jnp.exp2(scores * exp_scale)
        if diagonal:
            t = lax.rem(lax.broadcasted_iota(jnp.int32, (1, columns), 1), span)
            u = lax.broadcasted_iota(jnp.int32, (span, 1), 0)
            probs = jnp.where(u <= t, probs, 0.0)
        probs_b = probs.astype(BF16)
        shifted = nt(jnp.concatenate([v, minus], 1), jnp.concatenate([g, yg[query_half]], 1))
        dscores = (probs * shifted).astype(BF16)
        return nn(dscores, q), nn(probs_b, g), tn(k, dscores)

    pltpu.make_async_copy(qs, qs, load_sem.at[1]).wait()

    dk, dv, dq = unit(0, low, low, True)
    own[0, 0], own[1, 0], dqt[0] = dk, dv, dq
    dk, dv, dq = unit(0, low, high, False)
    own[0, 0] += dk
    own[1, 0] += dv
    dqt[1] = dq
    dk, dv, dq = unit(0, high, high, True)
    own[0, 1], own[1, 1] = dk, dv
    dqt[1] += dq

    def mark_in(slot):
        mark_puts[slot - 1].wait_recv()
        return pltpu.make_async_copy(marks.at[slot], mark_load.at[slot], mark_recv.at[slot])

    mark_loads = [mark_in(slot) for slot in range(1, REACH + 1)]
    for copy in mark_loads:
        copy.start()

    @pl.when(early)
    def _():
        reach_outer()

    for copy in mark_loads:
        copy.wait()

    targets = {1: mate, 2: inner_at(-2), 3: mate, 4: inner_at(-4), FAR: outer_at(-1)}
    term_put = {
        slot: remote(terms.at[slot], came.at[slot], term_send.at[slot], term_recv.at[slot], targets[slot])
        for slot in targets
    }

    def merge(slot, other):
        for at in range(2):
            for half in range(2):
                both = terms[slot, at, half].astype(F32) + came[other, at, half].astype(F32)
                terms[slot, at, half] = both.astype(BF16)

    soon = 1 - jnp.minimum(lax.rem(outer, 8), 1)

    def step(at_step, rest):
        slot, rest = lax.rem(rest, 8), rest // 8

        @pl.when(slot == FAR)
        def _():
            copy = mark_in(FAR)
            copy.start()
            copy.wait()

        @pl.when((at_step == 1) & (core == 1))
        def _():
            put4.wait_recv()
            put3.start()

        @pl.when((at_step == 2) & (core == 0))
        def _():
            put2.wait_recv()
            put3.start()

        @pl.when((at_step == 3 - soon) & (core == 1))
        def _():
            put2.wait_recv()
            put1.start()

        @pl.when((slot != 2) & (slot + core != 5))
        def _():
            put(0, slot, mate).wait_recv()

        @pl.when((slot == FAR) & (core == 0))
        def _():
            put5.wait_recv()

        there = mark_load[slot, 0, 0]
        there_low = jnp.where(there < n_outer * n_inner, 0, 1)
        run_here = jnp.minimum(first, 2 * n_outer * n_inner - 1 - first)
        run_there = jnp.minimum(there, 2 * n_outer * n_inner - 1 - there)
        earlier = run_there < run_here
        keep = jnp.where(earlier, 1.0, 0.0)
        dk, dv, dq = unit(slot, there_low, high, False)
        key_half = jnp.where(earlier, there_low, 1 - there_low)
        query_half = jnp.where(earlier, low, high)
        dk2, dv2, dq2 = unit(slot, key_half, query_half, False)
        dq_low = dq2 * keep
        dqt[0] += dq_low
        dqt[1] += dq + (dq2 - dq_low)
        for at, (one, two) in enumerate(((dk, dk2), (dv, dv2))):
            two_low = two * keep
            factor = 1.0 if at else scale
            terms[slot, at, 0] = ((one + two_low) * factor).astype(BF16)
            terms[slot, at, 1] = ((two - two_low) * factor).astype(BF16)

        @pl.when(slot == FAR)
        def _():
            term_put[FAR].start()

        @pl.when(slot == 1)
        def _():
            term_put[1].start()

        @pl.when(slot == 3)
        def _():
            term_put[3].start()

        @pl.when((slot == 4) & (core == 0))
        def _():
            term_put[4].start()

        @pl.when((slot == 3) & (core == 1))
        def _():
            term_put[3].wait_recv()
            merge(4, 3)
            term_put[4].start()

        @pl.when((slot == 2) & (core == 0))
        def _():
            term_put[3].wait_recv()
            merge(2, 3)
            term_put[2].start()

        @pl.when((slot == 2) & (core == 1))
        def _():
            term_put[1].wait_recv()
            merge(2, 1)
            term_put[2].start()

        return rest

    def packed(*order):
        return sum(slot * 8**at for at, slot in enumerate(order))

    orders = (
        (packed(FAR, 3, 4, 1, 2), packed(4, 3, 1, 2, FAR)),
        (packed(1, FAR, 4, 3, 2), packed(1, 4, 3, 2, FAR)),
    )
    even, odd = (late * (1 - soon) + ahead * soon for late, ahead in orders)
    lax.fori_loop(0, FAR, step, even * (1 - core) + odd * core)

    in_order = first < n_outer * n_inner
    dq_out = []
    for half in range(2):
        rank = jnp.where(in_order, half, 1 - half)
        rows = pl.ds(half * span, span)
        dq = (dqt[rank] * scale).T.astype(BF16)
        for h in range(heads):
            o_vm[rows, pl.ds(h * width, width)] = dq[h * span : (h + 1) * span]
        copy = pltpu.make_async_copy(o_vm.at[rows, :], dq_ref.at[rows, :], kv_sem.at[0, half])
        copy.start()
        dq_out.append(copy)

    @pl.when(core == 0)
    def _():
        term_put[1].wait_recv()

    for slot in (2, 4, FAR):
        term_put[slot].wait_recv()
    from_mate = jnp.where(core == 0, 1.0, 0.0)
    for at, out in enumerate((dk_ref, dv_ref)):
        for half in range(2):
            rank = jnp.where(in_order, half, 1 - half)
            total = own[at, rank] * (1.0 if at else scale) + came[1, at, rank].astype(F32) * from_mate
            for slot in (2, 4, FAR):
                total += came[slot, at, rank].astype(F32)
            out[pl.ds(half * span, span), :] = total.astype(BF16)

    for copy in mark_puts + [put1, put2, put3, put4, put5] + list(term_put.values()):
        copy.wait_send()
    for copy in dq_out:
        copy.wait()


def hand_over(*refs):
    count = len(refs) // 2
    copies = [
        pltpu.make_async_copy(refs[at], refs[count + at], refs[-1].at[at]) for at in range(count)
    ]
    for copy in copies:
        copy.start()
    for copy in copies:
        copy.wait()


def shards(queries, keys, values, saved_out, saved_lse, out_grad, positions):
    rows, columns = queries.shape
    width = keys.shape[1]
    span = rows // 2
    heads = columns // width
    anywhere = pl.BlockSpec(memory_space=pl.ANY)
    vmem = pl.BlockSpec(memory_space=pltpu.VMEM)
    slots = FAR + 1
    stack = (2, heads * span, width)
    pair = (2, 2, span, width)
    dma = pltpu.SemaphoreType.DMA
    results = pl.pallas_call(
        functools.partial(kernel, lax.axis_size("outer"), lax.axis_size("inner")),
        out_shape=(
            jax.ShapeDtypeStruct(queries.shape, BF16),
            jax.ShapeDtypeStruct(keys.shape, BF16),
            jax.ShapeDtypeStruct(values.shape, BF16),
        ),
        in_specs=[
            anywhere,
            anywhere,
            anywhere,
            anywhere,
            vmem,
            anywhere,
            pl.BlockSpec(memory_space=pltpu.SMEM),
        ],
        out_specs=[anywhere, vmem, vmem],
        scratch_shapes=[
            pltpu.VMEM(stack, BF16),
            pltpu.VMEM(stack, BF16),
            pltpu.VMEM(stack, BF16),
            pltpu.VMEM(stack, BF16),
            pltpu.VMEM((rows, columns), BF16),
            pltpu.VMEM((slots,) + pair, BF16),
            pltpu.VMEM((8, 128), jnp.int32),
            pltpu.VMEM((slots, 8, 128), jnp.int32),
            pltpu.VMEM((2, width, heads * span), F32),
            pltpu.VMEM(pair, F32),
            pltpu.VMEM((slots,) + pair, BF16),
            pltpu.VMEM((slots,) + pair, BF16),
            dma((3,)),
            dma((2, 2)),
            dma((slots,)),
            dma((slots,)),
            pltpu.SMEM((slots, 8, 128), jnp.int32),
            dma((slots,)),
            dma((slots,)),
            dma((slots,)),
            dma((slots,)),
            pltpu.SemaphoreType.REGULAR,
        ],
        compiler_params=pltpu.CompilerParams(
            collective_id=0, has_side_effects=True, vmem_limit_bytes=56 * 2**20
        ),
    )(queries, keys, values, saved_out, saved_lse.T, out_grad, positions)
    return pl.pallas_call(
        hand_over,
        out_shape=tuple(jax.ShapeDtypeStruct(x.shape, x.dtype) for x in results),
        in_specs=[anywhere] * 3,
        out_specs=[anywhere] * 3,
        scratch_shapes=[dma((3,))],
    )(*results)


def solution(mesh):
    rows = P(("outer", "inner"), None)
    return jax.shard_map(
        shards,
        mesh=mesh,
        in_specs=(rows,) * 6 + (P(("outer", "inner")),),
        out_specs=(rows,) * 3,
        check_vma=False,
    )
```

```python
import functools

import jax
import jax.numpy as jnp
import numpy as np
from jax import lax
from jax.experimental import pallas as pl
from jax.experimental.pallas import tpu as pltpu
from jax.sharding import PartitionSpec as P

F32 = jnp.float32
BF16 = jnp.bfloat16
REACH = 4
FAR = REACH + 1


def nn(a, b):
    return lax.dot_general(a, b, (((1,), (0,)), ((), ())), preferred_element_type=F32)


def nt(a, b):
    return lax.dot_general(a, b, (((1,), (1,)), ((), ())), preferred_element_type=F32)


def tn(a, b):
    return lax.dot_general(a, b, (((0,), (0,)), ((), ())), preferred_element_type=F32)


def kernel(
    n_outer,
    n_inner,
    q_hbm,
    k_hbm,
    v_hbm,
    o_hbm,
    lse_ref,
    g_hbm,
    pos_ref,
    dq_ref,
    dk_ref,
    dv_ref,
    qs,
    gs,
    yq,
    yg,
    o_vm,
    kv,
    mark,
    marks,
    dqt,
    own,
    terms,
    came,
    load_sem,
    kv_sem,
    mark_send,
    mark_recv,
    mark_load,
    put_sem,
    get_sem,
    term_send,
    term_recv,
    gate,
):
    outer = lax.axis_index("outer")
    inner = lax.axis_index("inner")
    span, width = kv.shape[3], kv.shape[4]
    heads = q_hbm.shape[1] // width
    scale = width**-0.5
    exp_scale = float(np.log2(np.e)) * scale
    core = lax.rem(inner, 2)
    side = lax.rem(inner // 2, 2)

    def inner_at(step):
        return (outer, lax.rem(inner + n_inner + step, n_inner))

    def outer_at(step):
        return (lax.rem(outer + n_outer + step, n_outer), inner)

    loads = []
    for src, dst in ((k_hbm, 0), (v_hbm, 1)):
        for half in range(2):
            copy = pltpu.make_async_copy(
                src.at[pl.ds(half * span, span), :], kv.at[0, dst, half], kv_sem.at[dst, half]
            )
            copy.start()
            loads.append(copy)

    def remote(src, dst, send_sem, recv_sem, target):
        return pltpu.make_async_remote_copy(
            src_ref=src,
            dst_ref=dst,
            send_sem=send_sem,
            recv_sem=recv_sem,
            device_id=target,
            device_id_type=pl.DeviceIdType.MESH,
        )

    def signal(semaphore, target):
        pl.semaphore_signal(semaphore, 1, device_id=target, device_id_type=pl.DeviceIdType.MESH)

    barrier = pltpu.get_barrier_semaphore()
    mate = (outer, inner + 1 - 2 * core)

    @pl.when(core == 0)
    def _():
        for step in (-4, -2, 2, 4):
            signal(barrier, inner_at(step))
        for step in (-1, 1):
            signal(barrier, (outer_at(step)[0], inner + 1))

    @pl.when(core == 1)
    def _():
        for step in (-5, -3, -1, 1, 3):
            signal(barrier, inner_at(step))
        for step in (-1, 1):
            signal(barrier, outer_at(step))

    for at, (src, dst) in enumerate(((g_hbm, gs), (q_hbm, qs))):
        for half in range(2):
            for h in range(heads):
                pltpu.make_async_copy(
                    src.at[pl.ds(half * span, span), pl.ds(h * width, width)],
                    dst.at[half, pl.ds(h * span, span), :],
                    load_sem.at[at],
                ).start()
        if at == 0:
            o_copy = pltpu.make_async_copy(o_hbm, o_vm, load_sem.at[2])
            o_copy.start()
    first = pos_ref[0] // span
    mark[...] = jnp.full(mark.shape, first, jnp.int32)
    for copy in loads:
        copy.wait()

    @pl.when(core == 0)
    def _():
        pl.semaphore_wait(barrier, 9)
        signal(gate, mate)

    @pl.when(core == 1)
    def _():
        pl.semaphore_wait(gate, 1)

    def put(src_slot, slot, target):
        return remote(kv.at[src_slot], kv.at[slot], put_sem.at[slot], get_sem.at[slot], target)

    put5 = put(0, FAR, outer_at(1))
    put4 = put(0, 4, inner_at(4))
    put2 = put(0, 2, inner_at(2))
    put1 = put(2 * core, 1, mate)
    put3 = put(2 + 2 * core, 3, mate)
    mark_puts = [
        remote(
            mark,
            marks.at[slot],
            mark_send.at[slot],
            mark_recv.at[slot],
            outer_at(1) if slot == FAR else inner_at(slot),
        )
        for slot in range(1, FAR + 1)
    ]
    for copy in mark_puts[:REACH]:
        copy.start()

    @pl.when(core == 0)
    def _():
        put1.start()
        put4.start()

    @pl.when(side == 0)
    def _():
        put2.start()

    def reach_outer():
        @pl.when(core == 1)
        def _():
            pl.semaphore_wait(barrier, 4)
            signal(gate, mate)

        @pl.when(core == 0)
        def _():
            pl.semaphore_wait(gate, 1)

        mark_puts[REACH].start()
        put5.start()

    early = lax.rem(outer, 8) == 0

    @pl.when(jnp.logical_not(early))
    def _():
        reach_outer()

    pltpu.make_async_copy(gs, gs, load_sem.at[0]).wait()
    o_copy.wait()
    lane = lax.broadcasted_iota(jnp.int32, (span, width), 1)
    spread = jnp.where(lane < 3 * heads, lax.rem(lane, heads), -1)

    def split(x):
        hi = x.astype(BF16).astype(F32)
        mid = (x - hi).astype(BF16).astype(F32)
        return jnp.where(lane < heads, hi, jnp.where(lane < 2 * heads, mid, x - hi - mid))

    norm_rows = jnp.concatenate(
        [lse_ref[...] * (1.0 / scale)] * 3 + [jnp.zeros((width - 3 * heads, 2 * span), F32)], 0
    )
    norm_table = norm_rows.T
    for half in range(2):
        rows = pl.ds(half * span, span)
        dots = jnp.zeros((span, width), F32)
        for h in range(heads):
            g = gs[half, pl.ds(h * span, span), :].astype(F32)
            o = o_vm[rows, pl.ds(h * width, width)].astype(F32)
            dots = jnp.where(spread == h, jnp.sum(g * o, axis=1, keepdims=True), dots)
        dots, norms = split(dots), split(norm_table[half * span : (half + 1) * span])
        for h in range(heads):
            to = pl.ds(h * span, span)
            yg[half, to, :] = jnp.where(spread == h, dots, 0.0).astype(BF16)
            yq[half, to, :] = jnp.where(spread == h, norms, 0.0).astype(BF16)

    @pl.when(core == 1)
    def _():
        put4.start()

    minus = jnp.where(lane < 3 * heads, -1.0, 0.0).astype(BF16)

    columns = heads * span
    high = jnp.where(first < n_outer * n_inner, 1, 0)
    low = 1 - high

    def unit(slot, key_half, query_half, diagonal):
        k, v = (lax.select(key_half == 1, kv[slot, at, 1], kv[slot, at, 0]) for at in range(2))
        q, g = qs[query_half], gs[query_half]
        scores = nt(jnp.concatenate([k, minus], 1), jnp.concatenate([q, yq[query_half]], 1))
        probs = jnp.exp2(scores * exp_scale)
        if diagonal:
            t = lax.rem(lax.broadcasted_iota(jnp.int32, (1, columns), 1), span)
            u = lax.broadcasted_iota(jnp.int32, (span, 1), 0)
            probs = jnp.where(u <= t, probs, 0.0)
        probs_b = probs.astype(BF16)
        shifted = nt(jnp.concatenate([v, minus], 1), jnp.concatenate([g, yg[query_half]], 1))
        dscores = (probs * shifted).astype(BF16)
        return nn(dscores, q), nn(probs_b, g), tn(k, dscores)

    pltpu.make_async_copy(qs, qs, load_sem.at[1]).wait()

    dk, dv, dq = unit(0, low, low, True)
    own[0, 0], own[1, 0], dqt[0] = dk, dv, dq
    dk, dv, dq = unit(0, low, high, False)
    own[0, 0] += dk
    own[1, 0] += dv
    dqt[1] = dq
    dk, dv, dq = unit(0, high, high, True)
    own[0, 1], own[1, 1] = dk, dv
    dqt[1] += dq

    def mark_in(slot):
        mark_puts[slot - 1].wait_recv()
        return pltpu.make_async_copy(marks.at[slot], mark_load.at[slot], mark_recv.at[slot])

    mark_loads = [mark_in(slot) for slot in range(1, REACH + 1)]
    for copy in mark_loads:
        copy.start()

    @pl.when(side == 1)
    def _():
        put2.start()

    @pl.when(early)
    def _():
        reach_outer()

    for copy in mark_loads:
        copy.wait()

    targets = {1: mate, 2: inner_at(-2), 3: inner_at(2 * core - 3), 4: inner_at(-4), FAR: outer_at(-1)}
    term_put = {
        slot: remote(terms.at[slot], came.at[slot], term_send.at[slot], term_recv.at[slot], targets[slot])
        for slot in targets
    }

    def merge(slot, other):
        for at in range(2):
            for half in range(2):
                both = terms[slot, at, half].astype(F32) + came[other, at, half].astype(F32)
                terms[slot, at, half] = both.astype(BF16)

    soon = 1 - jnp.minimum(lax.rem(outer, 8), 1)

    def step(at_step, rest):
        slot, rest = lax.rem(rest, 8), rest // 8

        @pl.when(slot == FAR)
        def _():
            copy = mark_in(FAR)
            copy.start()
            copy.wait()

        @pl.when((at_step == 1) & (core == 1))
        def _():
            put4.wait_recv()
            put3.start()

        @pl.when(at_step == 3 - soon)
        def _():
            put2.wait_recv()

        @pl.when((at_step == 3 - soon) & (core == 0))
        def _():
            put3.start()

        @pl.when((at_step == 3 - soon) & (core == 1))
        def _():
            put1.start()

        @pl.when(jnp.logical_not((slot == 2) | ((slot == 4) & (core == 1))))
        def _():
            put(0, slot, mate).wait_recv()

        there = mark_load[slot, 0, 0]
        there_low = jnp.where(there < n_outer * n_inner, 0, 1)
        run_here = jnp.minimum(first, 2 * n_outer * n_inner - 1 - first)
        run_there = jnp.minimum(there, 2 * n_outer * n_inner - 1 - there)
        earlier = run_there < run_here
        keep = jnp.where(earlier, 1.0, 0.0)
        dk, dv, dq = unit(slot, there_low, high, False)
        key_half = jnp.where(earlier, there_low, 1 - there_low)
        query_half = jnp.where(earlier, low, high)
        dk2, dv2, dq2 = unit(slot, key_half, query_half, False)
        dq_low = dq2 * keep
        dqt[0] += dq_low
        dqt[1] += dq + (dq2 - dq_low)
        for at, (one, two) in enumerate(((dk, dk2), (dv, dv2))):
            two_low = two * keep
            factor = 1.0 if at else scale
            terms[slot, at, 0] = ((one + two_low) * factor).astype(BF16)
            terms[slot, at, 1] = ((two - two_low) * factor).astype(BF16)

        for sent in (1, 3, 4, FAR):

            @pl.when(slot == sent)
            def _():
                term_put[sent].start()

        @pl.when((slot == 2) & (core == 0))
        def _():
            term_put[3].wait_recv()
            merge(2, 3)
            term_put[2].start()

        @pl.when((slot == 3) & (core == 1))
        def _():
            term_put[1].wait_recv()
            merge(2, 1)
            term_put[2].start()

        return rest

    def packed(*order):
        return sum(slot * 8**at for at, slot in enumerate(order))

    orders = (
        (packed(4, FAR, 3, 1, 2), packed(4, 3, 1, 2, FAR)),
        (packed(1, 4, FAR, 2, 3), packed(1, 4, 2, 3, FAR)),
    )
    even, odd = (late * (1 - soon) + ahead * soon for late, ahead in orders)
    lax.fori_loop(0, FAR, step, even * (1 - core) + odd * core)

    in_order = first < n_outer * n_inner
    dq_out = []
    for half in range(2):
        rank = jnp.where(in_order, half, 1 - half)
        rows = pl.ds(half * span, span)
        dq = (dqt[rank] * scale).T.astype(BF16)
        for h in range(heads):
            o_vm[rows, pl.ds(h * width, width)] = dq[h * span : (h + 1) * span]
        copy = pltpu.make_async_copy(o_vm.at[rows, :], dq_ref.at[rows, :], kv_sem.at[0, half])
        copy.start()
        dq_out.append(copy)

    @pl.when(core == 0)
    def _():
        term_put[1].wait_recv()

    @pl.when(core == 1)
    def _():
        term_put[3].wait_recv()

    for slot in (2, 4, FAR):
        term_put[slot].wait_recv()
    for at, out in enumerate((dk_ref, dv_ref)):
        for half in range(2):
            rank = jnp.where(in_order, half, 1 - half)
            total = own[at, rank] * (1.0 if at else scale)
            for slot in (1 + 2 * core, 2, 4, FAR):
                total += came[slot, at, rank].astype(F32)
            out[pl.ds(half * span, span), :] = total.astype(BF16)

    for copy in mark_puts + [put1, put2, put3, put4, put5] + list(term_put.values()):
        copy.wait_send()
    for copy in dq_out:
        copy.wait()


def hand_over(dq, dk, dv, dq_out, dk_out, dv_out, dq_vm, dk_vm, dv_vm, sem):
    rows = dq.shape[0] // 4
    parts = [pl.ds(at * rows, rows) for at in range(4)]
    routes = [(dq.at[part, :], dq_vm.at[part, :], dq_out.at[part, :]) for part in parts]
    routes += [(dk, dk_vm, dk_out), (dv, dv_vm, dv_out)]
    ins = [pltpu.make_async_copy(a, b, sem.at[0, at]) for at, (a, b, _) in enumerate(routes)]
    outs = [pltpu.make_async_copy(b, c, sem.at[1, at]) for at, (_, b, c) in enumerate(routes)]
    for copy in ins:
        copy.start()
    for came, goes in zip(ins, outs):
        came.wait()
        goes.start()
    for copy in outs:
        copy.wait()


def shards(queries, keys, values, saved_out, saved_lse, out_grad, positions):
    rows, columns = queries.shape
    width = keys.shape[1]
    span = rows // 2
    heads = columns // width
    anywhere = pl.BlockSpec(memory_space=pl.ANY)
    vmem = pl.BlockSpec(memory_space=pltpu.VMEM)
    slots = FAR + 1
    stack = (2, heads * span, width)
    pair = (2, 2, span, width)
    dma = pltpu.SemaphoreType.DMA
    results = pl.pallas_call(
        functools.partial(kernel, lax.axis_size("outer"), lax.axis_size("inner")),
        out_shape=(
            jax.ShapeDtypeStruct(queries.shape, BF16),
            jax.ShapeDtypeStruct(keys.shape, BF16),
            jax.ShapeDtypeStruct(values.shape, BF16),
        ),
        in_specs=[
            anywhere,
            anywhere,
            anywhere,
            anywhere,
            vmem,
            anywhere,
            pl.BlockSpec(memory_space=pltpu.SMEM),
        ],
        out_specs=[anywhere, vmem, vmem],
        scratch_shapes=[
            pltpu.VMEM(stack, BF16),
            pltpu.VMEM(stack, BF16),
            pltpu.VMEM(stack, BF16),
            pltpu.VMEM(stack, BF16),
            pltpu.VMEM((rows, columns), BF16),
            pltpu.VMEM((slots,) + pair, BF16),
            pltpu.VMEM((8, 128), jnp.int32),
            pltpu.VMEM((slots, 8, 128), jnp.int32),
            pltpu.VMEM((2, width, heads * span), F32),
            pltpu.VMEM(pair, F32),
            pltpu.VMEM((slots,) + pair, BF16),
            pltpu.VMEM((slots,) + pair, BF16),
            dma((3,)),
            dma((2, 2)),
            dma((slots,)),
            dma((slots,)),
            pltpu.SMEM((slots, 8, 128), jnp.int32),
            dma((slots,)),
            dma((slots,)),
            dma((slots,)),
            dma((slots,)),
            pltpu.SemaphoreType.REGULAR,
        ],
        compiler_params=pltpu.CompilerParams(
            collective_id=0, has_side_effects=True, vmem_limit_bytes=56 * 2**20
        ),
    )(queries, keys, values, saved_out, saved_lse.T, out_grad, positions)
    return pl.pallas_call(
        hand_over,
        out_shape=tuple(jax.ShapeDtypeStruct(x.shape, x.dtype) for x in results),
        in_specs=[anywhere] * 3,
        out_specs=[anywhere] * 3,
        scratch_shapes=[pltpu.VMEM(x.shape, x.dtype) for x in results] + [dma((2, 6))],
    )(*results)


def solution(mesh):
    rows = P(("outer", "inner"), None)
    return jax.shard_map(
        shards,
        mesh=mesh,
        in_specs=(rows,) * 6 + (P(("outer", "inner")),),
        out_specs=(rows,) * 3,
        check_vma=False,
    )
```

```python
import functools

import jax
import jax.numpy as jnp
import numpy as np
from jax import lax
from jax.experimental import pallas as pl
from jax.experimental.pallas import tpu as pltpu
from jax.sharding import PartitionSpec as P

F32 = jnp.float32
BF16 = jnp.bfloat16
REACH = 4
FAR = REACH + 1


def nn(a, b):
    return lax.dot_general(a, b, (((1,), (0,)), ((), ())), preferred_element_type=F32)


def nt(a, b):
    return lax.dot_general(a, b, (((1,), (1,)), ((), ())), preferred_element_type=F32)


def tn(a, b):
    return lax.dot_general(a, b, (((0,), (0,)), ((), ())), preferred_element_type=F32)


def kernel(
    n_outer,
    n_inner,
    q_hbm,
    k_hbm,
    v_hbm,
    o_hbm,
    lse_hbm,
    g_hbm,
    pos_hbm,
    dq_ref,
    dk_ref,
    dv_ref,
    qs,
    gs,
    yq,
    yg,
    o_vm,
    kv,
    mark,
    marks,
    dqt,
    own,
    terms,
    came,
    load_sem,
    kv_sem,
    mark_send,
    mark_recv,
    mark_load,
    put_sem,
    get_sem,
    term_send,
    term_recv,
    gate,
    lse_ref,
    pos_ref,
    small_sem,
):
    outer = lax.axis_index("outer")
    inner = lax.axis_index("inner")
    span, width = kv.shape[3], kv.shape[4]
    heads = q_hbm.shape[1] // width
    scale = width**-0.5
    exp_scale = float(np.log2(np.e)) * scale
    core = lax.rem(inner, 2)
    side = lax.rem(inner // 2, 2)

    def inner_at(step):
        return (outer, lax.rem(inner + n_inner + step, n_inner))

    def outer_at(step):
        return (lax.rem(outer + n_outer + step, n_outer), inner)

    def remote(src, dst, send_sem, recv_sem, target):
        return pltpu.make_async_remote_copy(
            src_ref=src,
            dst_ref=dst,
            send_sem=send_sem,
            recv_sem=recv_sem,
            device_id=target,
            device_id_type=pl.DeviceIdType.MESH,
        )

    def signal(semaphore, target):
        pl.semaphore_signal(semaphore, 1, device_id=target, device_id_type=pl.DeviceIdType.MESH)

    barrier = pltpu.get_barrier_semaphore()
    mate = (outer, inner + 1 - 2 * core)

    @pl.when(core == 0)
    def _():
        for step in (-4, -2, 2, 4):
            signal(barrier, inner_at(step))
        for step in (-1, 1):
            signal(barrier, (outer_at(step)[0], inner + 1))

    @pl.when(core == 1)
    def _():
        for step in (-5, -3, -1, 1, 3):
            signal(barrier, inner_at(step))
        for step in (-1, 1):
            signal(barrier, outer_at(step))

    loads = []
    for at, (src, dst) in enumerate(((pos_hbm, pos_ref), (lse_hbm, lse_ref))):
        copy = pltpu.make_async_copy(src, dst, small_sem.at[at])
        copy.start()
        loads.append(copy)
    for src, dst in ((k_hbm, 0), (v_hbm, 1)):
        for half in range(2):
            copy = pltpu.make_async_copy(
                src.at[pl.ds(half * span, span), :], kv.at[0, dst, half], kv_sem.at[dst, half]
            )
            copy.start()
            loads.append(copy)

    for at, (src, dst) in enumerate(((g_hbm, gs), (q_hbm, qs))):
        for half in range(2):
            for h in range(heads):
                pltpu.make_async_copy(
                    src.at[pl.ds(half * span, span), pl.ds(h * width, width)],
                    dst.at[half, pl.ds(h * span, span), :],
                    load_sem.at[at],
                ).start()
        if at == 0:
            o_copy = pltpu.make_async_copy(o_hbm, o_vm, load_sem.at[2])
            o_copy.start()
    for copy in loads:
        copy.wait()
    first = pos_ref[0] // span
    mark[...] = jnp.full(mark.shape, first, jnp.int32)

    @pl.when(core == 0)
    def _():
        pl.semaphore_wait(barrier, 9)
        signal(gate, mate)

    @pl.when(core == 1)
    def _():
        pl.semaphore_wait(gate, 1)

    def put(src_slot, slot, target):
        return remote(kv.at[src_slot], kv.at[slot], put_sem.at[slot], get_sem.at[slot], target)

    put5 = put(0, FAR, outer_at(1))
    put4 = put(0, 4, inner_at(4))
    put2 = put(0, 2, inner_at(2))
    put1 = put(2 * core, 1, mate)
    put3 = put(2 + 2 * core, 3, mate)
    mark_puts = [
        remote(
            mark,
            marks.at[slot],
            mark_send.at[slot],
            mark_recv.at[slot],
            outer_at(1) if slot == FAR else inner_at(slot),
        )
        for slot in range(1, FAR + 1)
    ]
    for copy in mark_puts[:REACH]:
        copy.start()

    @pl.when(core == 0)
    def _():
        put1.start()

    @pl.when((side == 0) & (core == 0))
    def _():
        put4.start()

    @pl.when((side == 0) | (core == 0))
    def _():
        put2.start()

    early = lax.rem(outer, 8) == 0

    def reach_outer():
        @pl.when(core == 1)
        def _():
            pl.semaphore_wait(barrier, 4)
            signal(gate, mate)

        @pl.when(core == 0)
        def _():
            pl.semaphore_wait(gate, 1)

        mark_puts[REACH].start()

        @pl.when(early | (core == 0))
        def _():
            put5.start()

    @pl.when(jnp.logical_not(early))
    def _():
        reach_outer()

    pltpu.make_async_copy(gs, gs, load_sem.at[0]).wait()
    o_copy.wait()
    lane = lax.broadcasted_iota(jnp.int32, (span, width), 1)
    spread = jnp.where(lane < 3 * heads, lax.rem(lane, heads), -1)

    def split(x):
        hi = x.astype(BF16).astype(F32)
        mid = (x - hi).astype(BF16).astype(F32)
        return jnp.where(lane < heads, hi, jnp.where(lane < 2 * heads, mid, x - hi - mid))

    norm_rows = jnp.concatenate(
        [lse_ref[...] * (1.0 / scale)] * 3 + [jnp.zeros((width - 3 * heads, 2 * span), F32)], 0
    )
    norm_table = norm_rows.T
    for half in range(2):
        rows = pl.ds(half * span, span)
        dots = jnp.zeros((span, width), F32)
        for h in range(heads):
            g = gs[half, pl.ds(h * span, span), :].astype(F32)
            o = o_vm[rows, pl.ds(h * width, width)].astype(F32)
            dots = jnp.where(spread == h, jnp.sum(g * o, axis=1, keepdims=True), dots)
        dots, norms = split(dots), split(norm_table[half * span : (half + 1) * span])
        for h in range(heads):
            to = pl.ds(h * span, span)
            yg[half, to, :] = jnp.where(spread == h, dots, 0.0).astype(BF16)
            yq[half, to, :] = jnp.where(spread == h, norms, 0.0).astype(BF16)

    minus = jnp.where(lane < 3 * heads, -1.0, 0.0).astype(BF16)

    columns = heads * span
    high = jnp.where(first < n_outer * n_inner, 1, 0)
    low = 1 - high

    def unit(slot, key_half, query_half, diagonal):
        k, v = (lax.select(key_half == 1, kv[slot, at, 1], kv[slot, at, 0]) for at in range(2))
        q, g = qs[query_half], gs[query_half]
        scores = nt(jnp.concatenate([k, minus], 1), jnp.concatenate([q, yq[query_half]], 1))
        probs = jnp.exp2(scores * exp_scale)
        if diagonal:
            t = lax.rem(lax.broadcasted_iota(jnp.int32, (1, columns), 1), span)
            u = lax.broadcasted_iota(jnp.int32, (span, 1), 0)
            probs = jnp.where(u <= t, probs, 0.0)
        probs_b = probs.astype(BF16)
        shifted = nt(jnp.concatenate([v, minus], 1), jnp.concatenate([g, yg[query_half]], 1))
        dscores = (probs * shifted).astype(BF16)
        return nn(dscores, q), nn(probs_b, g), tn(k, dscores)

    pltpu.make_async_copy(qs, qs, load_sem.at[1]).wait()

    dk, dv, dq = unit(0, low, low, True)
    own[0, 0], own[1, 0], dqt[0] = dk, dv, dq

    @pl.when((side == 0) & (core == 1))
    def _():
        put4.start()

    @pl.when((side == 1) & (core == 1))
    def _():
        put2.start()

    @pl.when(jnp.logical_not(early) & (core == 1))
    def _():
        put5.start()

    dk, dv, dq = unit(0, low, high, False)
    own[0, 0] += dk
    own[1, 0] += dv
    dqt[1] = dq
    dk, dv, dq = unit(0, high, high, True)
    own[0, 1], own[1, 1] = dk, dv
    dqt[1] += dq

    def mark_in(slot):
        mark_puts[slot - 1].wait_recv()
        return pltpu.make_async_copy(marks.at[slot], mark_load.at[slot], mark_recv.at[slot])

    mark_loads = [mark_in(slot) for slot in range(1, REACH + 1)]
    for copy in mark_loads:
        copy.start()

    @pl.when(side == 1)
    def _():
        put4.start()

    @pl.when(early)
    def _():
        reach_outer()

    for copy in mark_loads:
        copy.wait()

    targets = {1: mate, 2: inner_at(-2), 3: inner_at(2 * core - 3), 4: inner_at(-4), FAR: outer_at(-1)}
    term_put = {
        slot: remote(terms.at[slot], came.at[slot], term_send.at[slot], term_recv.at[slot], targets[slot])
        for slot in targets
    }

    def merge(slot, other):
        for at in range(2):
            for half in range(2):
                both = terms[slot, at, half].astype(F32) + came[other, at, half].astype(F32)
                terms[slot, at, half] = both.astype(BF16)

    def packed(*order):
        return sum(slot * 8**at for at, slot in enumerate(order))

    plans = (
        (packed(4, 1, 2, FAR, 3), 0, 9, 2),
        (packed(1, 4, 3, 2, FAR), 1, 1, 3),
        (packed(2, FAR, 1, 4, 3), 0, 9, 2),
        (packed(1, 2, 3, FAR, 4), 1, 4, 4),
        (packed(4, 1, 2, 3, FAR), 0, 9, 2),
        (packed(1, 4, 3, 2, FAR), 1, 1, 3),
        (packed(2, 1, 4, 3, FAR), 0, 9, 2),
        (packed(1, 2, 3, 4, FAR), 1, 3, 4),
    )
    role = 2 * side + core + 4 * (1 - jnp.minimum(lax.rem(outer, 8), 1))

    def planned(column):
        value = jnp.int32(plans[0][column])
        for at in range(1, len(plans)):
            value = jnp.where(role == at, plans[at][column], value)
        return value

    order, pass2_at, pass4_at, merge_at = (planned(column) for column in range(4))

    def step(at_step, rest):
        slot, rest = lax.rem(rest, 8), rest // 8

        @pl.when(slot == FAR)
        def _():
            copy = mark_in(FAR)
            copy.start()
            copy.wait()

        @pl.when(at_step == pass4_at)
        def _():
            put4.wait_recv()
            put3.start()

        @pl.when(at_step == pass2_at)
        def _():
            put2.wait_recv()

        @pl.when((at_step == pass2_at) & (core == 0))
        def _():
            put3.start()

        @pl.when((at_step == pass2_at) & (core == 1))
        def _():
            put1.start()

        @pl.when(jnp.logical_not((slot == 2) | ((slot == 4) & (core == 1))))
        def _():
            put(0, slot, mate).wait_recv()

        there = mark_load[slot, 0, 0]
        there_low = jnp.where(there < n_outer * n_inner, 0, 1)
        run_here = jnp.minimum(first, 2 * n_outer * n_inner - 1 - first)
        run_there = jnp.minimum(there, 2 * n_outer * n_inner - 1 - there)
        earlier = run_there < run_here
        keep = jnp.where(earlier, 1.0, 0.0)
        dk, dv, dq = unit(slot, there_low, high, False)
        key_half = jnp.where(earlier, there_low, 1 - there_low)
        query_half = jnp.where(earlier, low, high)
        dk2, dv2, dq2 = unit(slot, key_half, query_half, False)
        dq_low = dq2 * keep
        dqt[0] += dq_low
        dqt[1] += dq + (dq2 - dq_low)
        for at, (one, two) in enumerate(((dk, dk2), (dv, dv2))):
            two_low = two * keep
            factor = 1.0 if at else scale
            terms[slot, at, 0] = ((one + two_low) * factor).astype(BF16)
            terms[slot, at, 1] = ((two - two_low) * factor).astype(BF16)

        for sent in (1, 3, 4, FAR):

            @pl.when(slot == sent)
            def _():
                term_put[sent].start()

        @pl.when((at_step == merge_at) & (core == 0))
        def _():
            term_put[3].wait_recv()
            merge(2, 3)
            term_put[2].start()

        @pl.when((at_step == merge_at) & (core == 1))
        def _():
            term_put[1].wait_recv()
            merge(2, 1)
            term_put[2].start()

        return rest

    lax.fori_loop(0, FAR, step, order)

    in_order = first < n_outer * n_inner
    for half in range(2):
        rank = jnp.where(in_order, half, 1 - half)
        rows = pl.ds(half * span, span)
        dq = (dqt[rank] * scale).T.astype(BF16)
        for h in range(heads):
            dq_ref[rows, pl.ds(h * width, width)] = dq[h * span : (h + 1) * span]

    @pl.when(core == 0)
    def _():
        term_put[1].wait_recv()

    @pl.when(core == 1)
    def _():
        term_put[3].wait_recv()

    for slot in (2, 4, FAR):
        term_put[slot].wait_recv()
    for at, out in enumerate((dk_ref, dv_ref)):
        for half in range(2):
            rank = jnp.where(in_order, half, 1 - half)
            total = own[at, rank] * (1.0 if at else scale)
            for slot in (1 + 2 * core, 2, 4, FAR):
                total += came[slot, at, rank].astype(F32)
            out[pl.ds(half * span, span), :] = total.astype(BF16)

    for copy in mark_puts + [put1, put2, put3, put4, put5] + list(term_put.values()):
        copy.wait_send()


def shards(queries, keys, values, saved_out, saved_lse, out_grad, positions):
    rows, columns = queries.shape
    width = keys.shape[1]
    span = rows // 2
    heads = columns // width
    anywhere = pl.BlockSpec(memory_space=pl.ANY)
    vmem = pl.BlockSpec(memory_space=pltpu.VMEM)
    slots = FAR + 1
    stack = (2, heads * span, width)
    pair = (2, 2, span, width)
    dma = pltpu.SemaphoreType.DMA
    return pl.pallas_call(
        functools.partial(kernel, lax.axis_size("outer"), lax.axis_size("inner")),
        out_shape=(
            pltpu.VMEM(queries.shape, BF16),
            pltpu.VMEM(keys.shape, BF16),
            pltpu.VMEM(values.shape, BF16),
        ),
        in_specs=[anywhere] * 7,
        out_specs=[vmem] * 3,
        scratch_shapes=[
            pltpu.VMEM(stack, BF16),
            pltpu.VMEM(stack, BF16),
            pltpu.VMEM(stack, BF16),
            pltpu.VMEM(stack, BF16),
            pltpu.VMEM((rows, columns), BF16),
            pltpu.VMEM((slots,) + pair, BF16),
            pltpu.VMEM((8, 128), jnp.int32),
            pltpu.VMEM((slots, 8, 128), jnp.int32),
            pltpu.VMEM((2, width, heads * span), F32),
            pltpu.VMEM(pair, F32),
            pltpu.VMEM((slots,) + pair, BF16),
            pltpu.VMEM((slots,) + pair, BF16),
            dma((3,)),
            dma((2, 2)),
            dma((slots,)),
            dma((slots,)),
            pltpu.SMEM((slots, 8, 128), jnp.int32),
            dma((slots,)),
            dma((slots,)),
            dma((slots,)),
            dma((slots,)),
            pltpu.SemaphoreType.REGULAR,
            pltpu.VMEM((heads, rows), F32),
            pltpu.SMEM((rows,), jnp.int32),
            dma((2,)),
        ],
        compiler_params=pltpu.CompilerParams(
            collective_id=0, has_side_effects=True, vmem_limit_bytes=56 * 2**20
        ),
    )(queries, keys, values, saved_out, saved_lse.T, out_grad, positions)


def solution(mesh):
    rows = P(("outer", "inner"), None)
    return jax.shard_map(
        shards,
        mesh=mesh,
        in_specs=(rows,) * 6 + (P(("outer", "inner")),),
        out_specs=(rows,) * 3,
        check_vma=False,
    )
```

```python
import functools

import jax
import jax.numpy as jnp
import numpy as np
from jax import lax
from jax.experimental import pallas as pl
from jax.experimental.pallas import tpu as pltpu
from jax.sharding import PartitionSpec as P

F32 = jnp.float32
BF16 = jnp.bfloat16
REACH = 4
FAR = REACH + 1


def nn(a, b):
    return lax.dot_general(a, b, (((1,), (0,)), ((), ())), preferred_element_type=F32)


def nt(a, b):
    return lax.dot_general(a, b, (((1,), (1,)), ((), ())), preferred_element_type=F32)


def kernel(
    n_outer,
    n_inner,
    q_hbm,
    k_hbm,
    v_hbm,
    o_hbm,
    lse_hbm,
    g_hbm,
    pos_hbm,
    dq_ref,
    dk_ref,
    dv_ref,
    qs,
    gs,
    stats,
    o_vm,
    kv,
    mark,
    marks,
    dqt,
    own,
    terms,
    came,
    load_sem,
    kv_sem,
    mark_send,
    mark_recv,
    mark_load,
    put_sem,
    get_sem,
    term_send,
    term_recv,
    gate,
    lse_ref,
    pos_ref,
    small_sem,
):
    outer = lax.axis_index("outer")
    inner = lax.axis_index("inner")
    span, width = kv.shape[3], kv.shape[4]
    heads = q_hbm.shape[1] // width
    scale = width**-0.5
    exp_scale = float(np.log2(np.e)) * scale
    core = lax.rem(inner, 2)
    side = lax.rem(inner // 2, 2)

    def inner_at(step):
        return (outer, lax.rem(inner + n_inner + step, n_inner))

    def outer_at(step):
        return (lax.rem(outer + n_outer + step, n_outer), inner)

    def remote(src, dst, send_sem, recv_sem, target):
        return pltpu.make_async_remote_copy(
            src_ref=src,
            dst_ref=dst,
            send_sem=send_sem,
            recv_sem=recv_sem,
            device_id=target,
            device_id_type=pl.DeviceIdType.MESH,
        )

    def signal(semaphore, target):
        pl.semaphore_signal(semaphore, 1, device_id=target, device_id_type=pl.DeviceIdType.MESH)

    barrier = pltpu.get_barrier_semaphore()
    mate = (outer, inner + 1 - 2 * core)

    @pl.when(core == 0)
    def _():
        for step in (-4, -2, 2, 4):
            signal(barrier, inner_at(step))
        for step in (-1, 1):
            signal(barrier, (outer_at(step)[0], inner + 1))

    @pl.when(core == 1)
    def _():
        for step in (-5, -3, -1, 1, 3):
            signal(barrier, inner_at(step))
        for step in (-1, 1):
            signal(barrier, outer_at(step))

    loads = []
    for at, (src, dst) in enumerate(((pos_hbm, pos_ref), (lse_hbm, lse_ref))):
        copy = pltpu.make_async_copy(src, dst, small_sem.at[at])
        copy.start()
        loads.append(copy)
    for src, dst in ((k_hbm, 0), (v_hbm, 1)):
        for half in range(2):
            copy = pltpu.make_async_copy(
                src.at[pl.ds(half * span, span), :], kv.at[0, dst, half], kv_sem.at[dst, half]
            )
            copy.start()
            loads.append(copy)

    for at, (src, dst) in enumerate(((g_hbm, gs), (q_hbm, qs))):
        for half in range(2):
            for h in range(heads):
                pltpu.make_async_copy(
                    src.at[pl.ds(half * span, span), pl.ds(h * width, width)],
                    dst.at[half, pl.ds(h * span, span), :],
                    load_sem.at[at],
                ).start()
        if at == 0:
            o_copy = pltpu.make_async_copy(o_hbm, o_vm, load_sem.at[2])
            o_copy.start()
    for copy in loads:
        copy.wait()
    first = pos_ref[0] // span
    mark[...] = jnp.full(mark.shape, first, jnp.int32)

    @pl.when(core == 0)
    def _():
        pl.semaphore_wait(barrier, 9)
        signal(gate, mate)

    @pl.when(core == 1)
    def _():
        pl.semaphore_wait(gate, 1)

    def put(src_slot, slot, target):
        return remote(kv.at[src_slot], kv.at[slot], put_sem.at[slot], get_sem.at[slot], target)

    put5 = put(0, FAR, outer_at(1))
    put4 = put(0, 4, inner_at(4))
    put2 = put(0, 2, inner_at(2))
    put1 = put(2 * core, 1, mate)
    put3 = put(2 + 2 * core, 3, mate)
    mark_puts = [
        remote(
            mark,
            marks.at[slot],
            mark_send.at[slot],
            mark_recv.at[slot],
            outer_at(1) if slot == FAR else inner_at(slot),
        )
        for slot in range(1, FAR + 1)
    ]
    for copy in mark_puts[:REACH]:
        copy.start()

    @pl.when(core == 0)
    def _():
        put1.start()

    @pl.when((side == 0) & (core == 0))
    def _():
        put4.start()

    @pl.when(core == 0)
    def _():
        put2.start()

    early = lax.rem(outer, 8) == 0

    def reach_outer():
        @pl.when(core == 1)
        def _():
            pl.semaphore_wait(barrier, 4)
            signal(gate, mate)

        @pl.when(core == 0)
        def _():
            pl.semaphore_wait(gate, 1)

        mark_puts[REACH].start()

        @pl.when(early | (core == 0))
        def _():
            put5.start()

    @pl.when(jnp.logical_not(early))
    def _():
        reach_outer()

    pltpu.make_async_copy(gs, gs, load_sem.at[0]).wait()
    o_copy.wait()
    lane = lax.broadcasted_iota(jnp.int32, (span, width), 1)
    dots = []
    for half in range(2):
        table = jnp.zeros((span, width), F32)
        for h in range(heads):
            g = gs[half, pl.ds(h * span, span), :].astype(F32)
            o = o_vm[pl.ds(half * span, span), pl.ds(h * width, width)].astype(F32)
            table = jnp.where(lane == h, jnp.sum(g * o, axis=1, keepdims=True), table)
        dots.append(table)
    tables = (lse_ref[...] * float(np.log2(np.e)), jnp.concatenate(dots, 0).T)
    for at, table in enumerate(tables):
        for half in range(2):
            pieces = [table[h : h + 1, half * span : (half + 1) * span] for h in range(heads)]
            stats[at, half] = jnp.concatenate(pieces, 1)

    columns = heads * span
    high = jnp.where(first < n_outer * n_inner, 1, 0)
    low = 1 - high

    def unit(slot, key_half, query_half, diagonal):
        k, v = (lax.select(key_half == 1, kv[slot, at, 1], kv[slot, at, 0]) for at in range(2))
        q, g = qs[query_half], gs[query_half]
        probs = jnp.exp2(nt(k, q) * exp_scale - stats[0, query_half])
        if diagonal:
            t = lax.rem(lax.broadcasted_iota(jnp.int32, (1, columns), 1), span)
            u = lax.broadcasted_iota(jnp.int32, (span, 1), 0)
            probs = jnp.where(u <= t, probs, 0.0)
        probs_b = probs.astype(BF16)
        dscores = (probs * (nt(v, g) - stats[1, query_half])).astype(BF16)
        return nn(dscores, q), nn(probs_b, g), nn(k.T, dscores)

    pltpu.make_async_copy(qs, qs, load_sem.at[1]).wait()

    dk, dv, dq = unit(0, low, low, True)
    own[0, 0], own[1, 0], dqt[0] = dk, dv, dq

    @pl.when((side == 0) & (core == 1))
    def _():
        put4.start()

    @pl.when(core == 1)
    def _():
        put2.start()

    @pl.when(jnp.logical_not(early) & (core == 1))
    def _():
        put5.start()

    dk, dv, dq = unit(0, low, high, False)
    own[0, 0] += dk
    own[1, 0] += dv
    dqt[1] = dq
    def mark_load_of(slot):
        return pltpu.make_async_copy(marks.at[slot], mark_load.at[slot], mark_recv.at[slot])

    def mark_in(slot):
        mark_puts[slot - 1].wait_recv()
        return mark_load_of(slot)

    mark_loads = [mark_in(slot) for slot in range(1, REACH + 1)]
    for copy in mark_loads:
        copy.start()

    far_late = lax.rem(outer, 8) < 2

    @pl.when(jnp.logical_not(far_late))
    def _():
        mark_in(FAR).start()

    dk, dv, dq = unit(0, high, high, True)
    own[0, 1], own[1, 1] = dk, dv
    dqt[1] += dq

    @pl.when(side == 1)
    def _():
        put4.start()

    @pl.when(early)
    def _():
        reach_outer()

    for copy in mark_loads:
        copy.wait()

    @pl.when(jnp.logical_not(far_late))
    def _():
        mark_load_of(FAR).wait()

    targets = {1: mate, 2: inner_at(-2), 3: inner_at((1 - core) * (1 - 4 * side) - core), 4: inner_at(-4), FAR: outer_at(-1)}
    term_put = {
        slot: remote(terms.at[slot], came.at[slot], term_send.at[slot], term_recv.at[slot], targets[slot])
        for slot in targets
    }

    def merge(slot, other):
        for at in range(2):
            for half in range(2):
                both = terms[slot, at, half].astype(F32) + came[other, at, half].astype(F32)
                terms[slot, at, half] = both.astype(BF16)

    def packed(*order):
        return sum(slot * 8**at for at, slot in enumerate(order))

    plans = (
        (packed(4, 2, 3, 1, FAR), 0, 9, 2, 9),
        (packed(1, 3, 4, 2, FAR), 2, 1, 4, 3),
        (packed(2, FAR, 1, 4, 3), 0, 9, 2, 9),
        (packed(1, 3, 2, FAR, 4), 2, 4, 3, 9),
        (packed(4, 2, 3, 1, FAR), 0, 9, 2, 9),
        (packed(1, 3, 4, 2, FAR), 2, 1, 4, 3),
        (packed(2, 1, 4, 3, FAR), 0, 9, 2, 9),
        (packed(1, 3, 2, 4, FAR), 1, 3, 3, 9),
    )
    role = 2 * side + core + jnp.where(far_late, 4, 0)

    def planned(column):
        value = jnp.int32(plans[0][column])
        for at in range(1, len(plans)):
            value = jnp.where(role == at, plans[at][column], value)
        return value

    order, pass2_at, pass4_at, merge2_at, merge4_at = (planned(column) for column in range(5))

    def step(at_step, rest):
        slot, rest = lax.rem(rest, 8), rest // 8

        @pl.when((slot == FAR) & far_late)
        def _():
            copy = mark_in(FAR)
            copy.start()
            copy.wait()

        @pl.when(at_step == pass4_at)
        def _():
            put4.wait_recv()
            put3.start()

        @pl.when(at_step == pass2_at)
        def _():
            put2.wait_recv()

        @pl.when((at_step == pass2_at) & (core == 0))
        def _():
            put3.start()

        @pl.when((at_step == pass2_at) & (core == 1))
        def _():
            put1.start()

        @pl.when(jnp.logical_not((slot == 2) | ((slot == 4) & (core == 1))))
        def _():
            put(0, slot, mate).wait_recv()

        there = mark_load[slot, 0, 0]
        there_low = jnp.where(there < n_outer * n_inner, 0, 1)
        run_here = jnp.minimum(first, 2 * n_outer * n_inner - 1 - first)
        run_there = jnp.minimum(there, 2 * n_outer * n_inner - 1 - there)
        earlier = run_there < run_here
        keep = jnp.where(earlier, 1.0, 0.0)
        dk, dv, dq = unit(slot, there_low, high, False)
        key_half = jnp.where(earlier, there_low, 1 - there_low)
        query_half = jnp.where(earlier, low, high)
        dk2, dv2, dq2 = unit(slot, key_half, query_half, False)
        dq_low = dq2 * keep
        dqt[0] += dq_low
        dqt[1] += dq + (dq2 - dq_low)
        for at, (one, two) in enumerate(((dk, dk2), (dv, dv2))):
            two_low = two * keep
            factor = 1.0 if at else scale
            terms[slot, at, 0] = ((one + two_low) * factor).astype(BF16)
            terms[slot, at, 1] = ((two - two_low) * factor).astype(BF16)

        for sent in (1, 3, FAR):

            @pl.when(slot == sent)
            def _():
                term_put[sent].start()

        @pl.when((slot == 4) & ((side == 1) | (core == 0)))
        def _():
            term_put[4].start()

        @pl.when(at_step == merge4_at)
        def _():
            term_put[3].wait_recv()
            merge(4, 3)
            term_put[4].start()

        @pl.when((at_step == merge2_at) & (core == 0))
        def _():
            term_put[3].wait_recv()
            merge(2, 3)
            term_put[2].start()

        @pl.when((at_step == merge2_at) & (core == 1))
        def _():
            term_put[1].wait_recv()
            merge(2, 1)
            term_put[2].start()

        return rest

    lax.fori_loop(0, FAR, step, order)

    in_order = first < n_outer * n_inner
    for half in range(2):
        rank = jnp.where(in_order, half, 1 - half)
        rows = pl.ds(half * span, span)
        dq = (dqt[rank] * scale).T.astype(BF16)
        for h in range(heads):
            dq_ref[rows, pl.ds(h * width, width)] = dq[h * span : (h + 1) * span]

    @pl.when(core == 0)
    def _():
        term_put[1].wait_recv()

    @pl.when((core == 1) & (side == 1))
    def _():
        term_put[3].wait_recv()

    direct = jnp.where((core == 0) | (side == 1), 1.0, 0.0)
    for slot in (2, 4, FAR):
        term_put[slot].wait_recv()
    for at, out in enumerate((dk_ref, dv_ref)):
        for half in range(2):
            rank = jnp.where(in_order, half, 1 - half)
            total = own[at, rank] * (1.0 if at else scale)
            total += came[1 + 2 * core, at, rank].astype(F32) * direct
            for slot in (2, 4, FAR):
                total += came[slot, at, rank].astype(F32)
            out[pl.ds(half * span, span), :] = total.astype(BF16)

    for copy in mark_puts + [put1, put2, put3, put4, put5] + list(term_put.values()):
        copy.wait_send()


def shards(queries, keys, values, saved_out, saved_lse, out_grad, positions):
    rows, columns = queries.shape
    width = keys.shape[1]
    span = rows // 2
    heads = columns // width
    anywhere = pl.BlockSpec(memory_space=pl.ANY)
    vmem = pl.BlockSpec(memory_space=pltpu.VMEM)
    slots = FAR + 1
    stack = (2, heads * span, width)
    pair = (2, 2, span, width)
    dma = pltpu.SemaphoreType.DMA
    return pl.pallas_call(
        functools.partial(kernel, lax.axis_size("outer"), lax.axis_size("inner")),
        out_shape=(
            pltpu.VMEM(queries.shape, BF16),
            pltpu.VMEM(keys.shape, BF16),
            pltpu.VMEM(values.shape, BF16),
        ),
        in_specs=[anywhere] * 7,
        out_specs=[vmem] * 3,
        scratch_shapes=[
            pltpu.VMEM(stack, BF16),
            pltpu.VMEM(stack, BF16),
            pltpu.VMEM((2, 2, 1, heads * span), F32),
            pltpu.VMEM((rows, columns), BF16),
            pltpu.VMEM((slots,) + pair, BF16),
            pltpu.VMEM((8, 128), jnp.int32),
            pltpu.VMEM((slots, 8, 128), jnp.int32),
            pltpu.VMEM((2, width, heads * span), F32),
            pltpu.VMEM(pair, F32),
            pltpu.VMEM((slots,) + pair, BF16),
            pltpu.VMEM((slots,) + pair, BF16),
            dma((3,)),
            dma((2, 2)),
            dma((slots,)),
            dma((slots,)),
            pltpu.SMEM((slots, 8, 128), jnp.int32),
            dma((slots,)),
            dma((slots,)),
            dma((slots,)),
            dma((slots,)),
            pltpu.SemaphoreType.REGULAR,
            pltpu.VMEM((heads, rows), F32),
            pltpu.SMEM((rows,), jnp.int32),
            dma((2,)),
        ],
        compiler_params=pltpu.CompilerParams(
            collective_id=0, has_side_effects=True, vmem_limit_bytes=56 * 2**20
        ),
    )(queries, keys, values, saved_out, saved_lse.T, out_grad, positions)


def solution(mesh):
    rows = P(("outer", "inner"), None)
    return jax.shard_map(
        shards,
        mesh=mesh,
        in_specs=(rows,) * 6 + (P(("outer", "inner")),),
        out_specs=(rows,) * 3,
        check_vma=False,
    )
```

```python
import functools

import jax
import jax.numpy as jnp
import numpy as np
from jax import lax
from jax.experimental import pallas as pl
from jax.experimental.pallas import tpu as pltpu
from jax.sharding import PartitionSpec as P

F32 = jnp.float32
BF16 = jnp.bfloat16
REACH = 4
FAR = REACH + 1


def nn(a, b):
    return lax.dot_general(a, b, (((1,), (0,)), ((), ())), preferred_element_type=F32)


def nt(a, b):
    return lax.dot_general(a, b, (((1,), (1,)), ((), ())), preferred_element_type=F32)


def kernel(
    n_outer,
    n_inner,
    q_hbm,
    k_hbm,
    v_hbm,
    o_hbm,
    lse_hbm,
    g_hbm,
    pos_hbm,
    out_ref,
    qs,
    gs,
    stats,
    o_vm,
    kv,
    mark,
    marks,
    dqt,
    own,
    terms,
    came,
    load_sem,
    kv_sem,
    mark_send,
    mark_recv,
    mark_load,
    put_sem,
    get_sem,
    term_send,
    term_recv,
    gate,
    lse_ref,
    pos_ref,
    small_sem,
):
    outer = lax.axis_index("outer")
    inner = lax.axis_index("inner")
    span, width = kv.shape[3], kv.shape[4]
    heads = q_hbm.shape[1] // width
    scale = width**-0.5
    exp_scale = float(np.log2(np.e)) * scale
    core = lax.rem(inner, 2)
    side = lax.rem(inner // 2, 2)

    def inner_at(step):
        return (outer, lax.rem(inner + n_inner + step, n_inner))

    def outer_at(step):
        return (lax.rem(outer + n_outer + step, n_outer), inner)

    def remote(src, dst, send_sem, recv_sem, target):
        return pltpu.make_async_remote_copy(
            src_ref=src,
            dst_ref=dst,
            send_sem=send_sem,
            recv_sem=recv_sem,
            device_id=target,
            device_id_type=pl.DeviceIdType.MESH,
        )

    def signal(semaphore, target):
        pl.semaphore_signal(semaphore, 1, device_id=target, device_id_type=pl.DeviceIdType.MESH)

    barrier = pltpu.get_barrier_semaphore()
    mate = (outer, inner + 1 - 2 * core)

    @pl.when(core == 0)
    def _():
        for step in (-4, -2, 2, 4):
            signal(barrier, inner_at(step))
        for step in (-1, 1):
            signal(barrier, (outer_at(step)[0], inner + 1))

    @pl.when(core == 1)
    def _():
        for step in (-5, -3, -1, 1, 3):
            signal(barrier, inner_at(step))
        for step in (-1, 1):
            signal(barrier, outer_at(step))

    loads = []
    for at, (src, dst) in enumerate(((pos_hbm, pos_ref), (lse_hbm, lse_ref))):
        copy = pltpu.make_async_copy(src, dst, small_sem.at[at])
        copy.start()
        loads.append(copy)
    for src, dst in ((k_hbm, 0), (v_hbm, 1)):
        for half in range(2):
            copy = pltpu.make_async_copy(
                src.at[pl.ds(half * span, span), :], kv.at[0, dst, half], kv_sem.at[dst, half]
            )
            copy.start()
            loads.append(copy)

    for at, (src, dst) in enumerate(((g_hbm, gs), (q_hbm, qs))):
        for half in range(2):
            for h in range(heads):
                pltpu.make_async_copy(
                    src.at[pl.ds(half * span, span), pl.ds(h * width, width)],
                    dst.at[half, pl.ds(h * span, span), :],
                    load_sem.at[at],
                ).start()
        if at == 0:
            o_copy = pltpu.make_async_copy(o_hbm, o_vm, load_sem.at[2])
            o_copy.start()
    for copy in loads:
        copy.wait()
    first = pos_ref[0] // span
    mark[...] = jnp.full(mark.shape, first, jnp.int32)

    @pl.when(core == 0)
    def _():
        pl.semaphore_wait(barrier, 9)
        signal(gate, mate)

    @pl.when(core == 1)
    def _():
        pl.semaphore_wait(gate, 1)

    def put(src_slot, slot, target):
        return remote(kv.at[src_slot], kv.at[slot], put_sem.at[slot], get_sem.at[slot], target)

    put5 = put(0, FAR, outer_at(1))
    put4 = put(0, 4, inner_at(4))
    put2 = put(0, 2, inner_at(2))
    put1 = put(2 * core, 1, mate)
    put3 = put(2 + 2 * core, 3, mate)
    mark_puts = [
        remote(
            mark,
            marks.at[slot],
            mark_send.at[slot],
            mark_recv.at[slot],
            outer_at(1) if slot == FAR else inner_at(slot),
        )
        for slot in range(1, FAR + 1)
    ]
    for copy in mark_puts[:REACH]:
        copy.start()

    @pl.when(core == 0)
    def _():
        put1.start()

    @pl.when((side == 0) & (core == 0))
    def _():
        put4.start()

    @pl.when(core == 0)
    def _():
        put2.start()

    early = lax.rem(outer, 8) == 0
    last = lax.rem(outer, 8) == 7

    def reach_outer():
        @pl.when(core == 1)
        def _():
            pl.semaphore_wait(barrier, 4)
            signal(gate, mate)

        @pl.when(core == 0)
        def _():
            pl.semaphore_wait(gate, 1)

        mark_puts[REACH].start()

        @pl.when(early | last | (core == 0))
        def _():
            put5.start()

    @pl.when(jnp.logical_not(early))
    def _():
        reach_outer()

    pltpu.make_async_copy(gs, gs, load_sem.at[0]).wait()
    o_copy.wait()
    lane = lax.broadcasted_iota(jnp.int32, (span, width), 1)
    dots = []
    for half in range(2):
        table = jnp.zeros((span, width), F32)
        for h in range(heads):
            g = gs[half, pl.ds(h * span, span), :].astype(F32)
            o = o_vm[pl.ds(half * span, span), pl.ds(h * width, width)].astype(F32)
            table = jnp.where(lane == h, jnp.sum(g * o, axis=1, keepdims=True), table)
        dots.append(table)
    tables = (lse_ref[...] * float(np.log2(np.e)), jnp.concatenate(dots, 0).T)
    for at, table in enumerate(tables):
        for half in range(2):
            pieces = [table[h : h + 1, half * span : (half + 1) * span] for h in range(heads)]
            stats[at, half] = jnp.concatenate(pieces, 1)

    columns = heads * span
    high = jnp.where(first < n_outer * n_inner, 1, 0)
    low = 1 - high

    def unit(slot, key_half, query_half, diagonal):
        k, v = (lax.select(key_half == 1, kv[slot, at, 1], kv[slot, at, 0]) for at in range(2))
        q, g = qs[query_half], gs[query_half]
        probs = jnp.exp2(nt(k, q) * exp_scale - stats[0, query_half])
        if diagonal:
            t = lax.rem(lax.broadcasted_iota(jnp.int32, (1, columns), 1), span)
            u = lax.broadcasted_iota(jnp.int32, (span, 1), 0)
            probs = jnp.where(u <= t, probs, 0.0)
        probs_b = probs.astype(BF16)
        dscores = (probs * (nt(v, g) - stats[1, query_half])).astype(BF16)
        return nn(dscores, q), nn(probs_b, g), nn(k.T, dscores)

    pltpu.make_async_copy(qs, qs, load_sem.at[1]).wait()

    dk, dv, dq = unit(0, low, low, True)
    own[0, 0], own[1, 0], dqt[0] = dk, dv, dq

    @pl.when((side == 0) & (core == 1))
    def _():
        put4.start()

    @pl.when(core == 1)
    def _():
        put2.start()

    @pl.when(jnp.logical_not(early | last) & (core == 1))
    def _():
        put5.start()

    dk, dv, dq = unit(0, low, high, False)
    own[0, 0] += dk
    own[1, 0] += dv
    dqt[1] = dq

    @pl.when(side == 1)
    def _():
        put4.start()

    def mark_load_of(slot):
        return pltpu.make_async_copy(marks.at[slot], mark_load.at[slot], mark_recv.at[slot])

    def mark_in(slot):
        mark_puts[slot - 1].wait_recv()
        return mark_load_of(slot)

    mark_loads = [mark_in(slot) for slot in range(1, REACH + 1)]
    for copy in mark_loads:
        copy.start()

    far_late = lax.rem(outer, 8) < 2

    @pl.when(jnp.logical_not(far_late))
    def _():
        mark_in(FAR).start()

    dk, dv, dq = unit(0, high, high, True)
    own[0, 1], own[1, 1] = dk, dv
    dqt[1] += dq


    @pl.when(early)
    def _():
        reach_outer()

    for copy in mark_loads:
        copy.wait()

    @pl.when(jnp.logical_not(far_late))
    def _():
        mark_load_of(FAR).wait()

    targets = {1: mate, 2: inner_at(-2), 3: inner_at((1 - core) * (1 - 4 * side) - core), 4: inner_at(-4), FAR: outer_at(-1)}
    term_put = {
        slot: remote(terms.at[slot], came.at[slot], term_send.at[slot], term_recv.at[slot], targets[slot])
        for slot in targets
    }

    def merge(slot, other):
        for at in range(2):
            for half in range(2):
                both = terms[slot, at, half].astype(F32) + came[other, at, half].astype(F32)
                terms[slot, at, half] = both.astype(BF16)

    def packed(*order):
        return sum(slot * 8**at for at, slot in enumerate(order))

    plans = (
        (packed(4, 2, 3, 1, FAR), 0, 9, 2, 9),
        (packed(1, 3, FAR, 4, 2), 2, 1, 4, 3),
        (packed(2, FAR, 1, 4, 3), 0, 9, 2, 9),
        (packed(1, 3, 2, FAR, 4), 2, 4, 3, 9),
        (packed(4, 2, 3, 1, FAR), 0, 9, 2, 9),
        (packed(1, 3, 4, 2, FAR), 2, 1, 4, 3),
        (packed(2, 1, 4, 3, FAR), 0, 9, 2, 9),
        (packed(1, 3, 2, 4, FAR), 1, 3, 3, 9),
        (packed(4, 2, 3, FAR, 1), 0, 9, 2, 9),
        (packed(1, 3, FAR, 4, 2), 2, 1, 4, 3),
        (packed(2, 1, FAR, 4, 3), 0, 9, 2, 9),
        (packed(1, 3, 2, FAR, 4), 2, 4, 3, 9),
    )
    role = 2 * side + core + jnp.where(early, 4, 0) + jnp.where(lax.rem(outer, 8) == 1, 8, 0)

    def planned(column):
        value = jnp.int32(plans[0][column])
        for at in range(1, len(plans)):
            value = jnp.where(role == at, plans[at][column], value)
        return value

    order, pass2_at, pass4_at, merge2_at, merge4_at = (planned(column) for column in range(5))

    def step(at_step, rest):
        slot, rest = lax.rem(rest, 8), rest // 8

        @pl.when((slot == FAR) & far_late)
        def _():
            copy = mark_in(FAR)
            copy.start()
            copy.wait()

        @pl.when(at_step == pass4_at)
        def _():
            put4.wait_recv()
            put3.start()

        @pl.when(at_step == pass2_at)
        def _():
            put2.wait_recv()

        @pl.when((at_step == pass2_at) & (core == 0))
        def _():
            put3.start()

        @pl.when((at_step == pass2_at) & (core == 1))
        def _():
            put1.start()

        @pl.when(jnp.logical_not((slot == 2) | ((slot == 4) & (core == 1))))
        def _():
            put(0, slot, mate).wait_recv()

        there = mark_load[slot, 0, 0]
        there_low = jnp.where(there < n_outer * n_inner, 0, 1)
        run_here = jnp.minimum(first, 2 * n_outer * n_inner - 1 - first)
        run_there = jnp.minimum(there, 2 * n_outer * n_inner - 1 - there)
        earlier = run_there < run_here
        keep = jnp.where(earlier, 1.0, 0.0)
        dk, dv, dq = unit(slot, there_low, high, False)
        key_half = jnp.where(earlier, there_low, 1 - there_low)
        query_half = jnp.where(earlier, low, high)
        dk2, dv2, dq2 = unit(slot, key_half, query_half, False)
        dq_low = dq2 * keep
        dqt[0] += dq_low
        dqt[1] += dq + (dq2 - dq_low)
        for at, (one, two) in enumerate(((dk, dk2), (dv, dv2))):
            two_low = two * keep
            factor = 1.0 if at else scale
            terms[slot, at, 0] = ((one + two_low) * factor).astype(BF16)
            terms[slot, at, 1] = ((two - two_low) * factor).astype(BF16)

        for sent in (1, 3, FAR):

            @pl.when(slot == sent)
            def _():
                term_put[sent].start()

        @pl.when((slot == 4) & ((side == 1) | (core == 0)))
        def _():
            term_put[4].start()

        @pl.when(at_step == merge4_at)
        def _():
            term_put[3].wait_recv()
            merge(4, 3)
            term_put[4].start()

        @pl.when((at_step == merge2_at) & (core == 0))
        def _():
            term_put[3].wait_recv()
            merge(2, 3)
            term_put[2].start()

        @pl.when((at_step == merge2_at) & (core == 1))
        def _():
            term_put[1].wait_recv()
            merge(2, 1)
            term_put[2].start()

        return rest

    lax.fori_loop(0, FAR, step, order)

    in_order = first < n_outer * n_inner
    for half in range(2):
        rank = jnp.where(in_order, half, 1 - half)
        rows = pl.ds(half * span, span)
        dq = (dqt[rank] * scale).T.astype(BF16)
        for h in range(heads):
            out_ref[rows, pl.ds(h * width, width)] = dq[h * span : (h + 1) * span]

    @pl.when(core == 0)
    def _():
        term_put[1].wait_recv()

    @pl.when((core == 1) & (side == 1))
    def _():
        term_put[3].wait_recv()

    direct = jnp.where((core == 0) | (side == 1), 1.0, 0.0)
    for slot in (2, 4, FAR):
        term_put[slot].wait_recv()
    for at in range(2):
        for half in range(2):
            rank = jnp.where(in_order, half, 1 - half)
            total = own[at, rank] * (1.0 if at else scale)
            total += came[1 + 2 * core, at, rank].astype(F32) * direct
            for slot in (2, 4, FAR):
                total += came[slot, at, rank].astype(F32)
            out_ref[pl.ds(half * span, span), pl.ds((heads + at) * width, width)] = total.astype(BF16)

    for copy in mark_puts + [put1, put2, put3, put4, put5] + list(term_put.values()):
        copy.wait_send()


def shards(queries, keys, values, saved_out, saved_lse, out_grad, positions):
    rows, columns = queries.shape
    width = keys.shape[1]
    span = rows // 2
    heads = columns // width
    anywhere = pl.BlockSpec(memory_space=pl.ANY)
    vmem = pl.BlockSpec(memory_space=pltpu.VMEM)
    slots = FAR + 1
    stack = (2, heads * span, width)
    pair = (2, 2, span, width)
    dma = pltpu.SemaphoreType.DMA
    grads = pl.pallas_call(
        functools.partial(kernel, lax.axis_size("outer"), lax.axis_size("inner")),
        out_shape=pltpu.VMEM((rows, columns + 2 * width), BF16),
        in_specs=[anywhere] * 7,
        out_specs=vmem,
        scratch_shapes=[
            pltpu.VMEM(stack, BF16),
            pltpu.VMEM(stack, BF16),
            pltpu.VMEM((2, 2, 1, heads * span), F32),
            pltpu.VMEM((rows, columns), BF16),
            pltpu.VMEM((slots,) + pair, BF16),
            pltpu.VMEM((8, 128), jnp.int32),
            pltpu.VMEM((slots, 8, 128), jnp.int32),
            pltpu.VMEM((2, width, heads * span), F32),
            pltpu.VMEM(pair, F32),
            pltpu.VMEM((slots,) + pair, BF16),
            pltpu.VMEM((slots,) + pair, BF16),
            dma((3,)),
            dma((2, 2)),
            dma((slots,)),
            dma((slots,)),
            pltpu.SMEM((slots, 8, 128), jnp.int32),
            dma((slots,)),
            dma((slots,)),
            dma((slots,)),
            dma((slots,)),
            pltpu.SemaphoreType.REGULAR,
            pltpu.VMEM((heads, rows), F32),
            pltpu.SMEM((rows,), jnp.int32),
            dma((2,)),
        ],
        compiler_params=pltpu.CompilerParams(
            collective_id=0, has_side_effects=True, vmem_limit_bytes=56 * 2**20
        ),
    )(queries, keys, values, saved_out, saved_lse.T, out_grad, positions)
    return grads[:, :columns], grads[:, columns : columns + width], grads[:, columns + width :]


def solution(mesh):
    rows = P(("outer", "inner"), None)
    return jax.shard_map(
        shards,
        mesh=mesh,
        in_specs=(rows,) * 6 + (P(("outer", "inner")),),
        out_specs=(rows,) * 3,
        check_vma=False,
    )
```

```python
import functools

import jax
import jax.numpy as jnp
import numpy as np
from jax import lax
from jax.experimental import pallas as pl
from jax.experimental.pallas import tpu as pltpu
from jax.sharding import PartitionSpec as P

F32 = jnp.float32
BF16 = jnp.bfloat16
REACH = 4
FAR = REACH + 1


def nn(a, b):
    return lax.dot_general(a, b, (((1,), (0,)), ((), ())), preferred_element_type=F32)


def nt(a, b):
    return lax.dot_general(a, b, (((1,), (1,)), ((), ())), preferred_element_type=F32)


def kernel(
    n_outer,
    n_inner,
    q_hbm,
    k_hbm,
    v_hbm,
    o_hbm,
    lse_hbm,
    g_hbm,
    pos_hbm,
    out_ref,
    qs,
    gs,
    stats,
    o_vm,
    kv,
    mark,
    marks,
    dqt,
    own,
    terms,
    came,
    load_sem,
    kv_sem,
    mark_send,
    mark_recv,
    mark_load,
    put_sem,
    get_sem,
    term_send,
    term_recv,
    gate,
    lse_ref,
    pos_ref,
    small_sem,
):
    outer = lax.axis_index("outer")
    inner = lax.axis_index("inner")
    span, width = kv.shape[3], kv.shape[4]
    heads = q_hbm.shape[1] // width
    scale = width**-0.5
    exp_scale = float(np.log2(np.e)) * scale
    core = lax.rem(inner, 2)
    side = lax.rem(inner // 2, 2)

    def inner_at(step):
        return (outer, lax.rem(inner + n_inner + step, n_inner))

    def outer_at(step):
        return (lax.rem(outer + n_outer + step, n_outer), inner)

    def remote(src, dst, send_sem, recv_sem, target):
        return pltpu.make_async_remote_copy(
            src_ref=src,
            dst_ref=dst,
            send_sem=send_sem,
            recv_sem=recv_sem,
            device_id=target,
            device_id_type=pl.DeviceIdType.MESH,
        )

    def signal(semaphore, target):
        pl.semaphore_signal(semaphore, 1, device_id=target, device_id_type=pl.DeviceIdType.MESH)

    barrier = pltpu.get_barrier_semaphore()
    mate = (outer, inner + 1 - 2 * core)

    @pl.when(core == 0)
    def _():
        for step in (-4, -2, 2, 4):
            signal(barrier, inner_at(step))
        for step in (-1, 1):
            signal(barrier, (outer_at(step)[0], inner + 1))

    @pl.when(core == 1)
    def _():
        for step in (-5, -3, -1, 1, 3):
            signal(barrier, inner_at(step))
        for step in (-1, 1):
            signal(barrier, outer_at(step))

    loads = []
    for at, (src, dst) in enumerate(((pos_hbm, pos_ref), (lse_hbm, lse_ref))):
        copy = pltpu.make_async_copy(src, dst, small_sem.at[at])
        copy.start()
        loads.append(copy)
    for src, dst in ((k_hbm, 0), (v_hbm, 1)):
        for half in range(2):
            copy = pltpu.make_async_copy(
                src.at[pl.ds(half * span, span), :], kv.at[0, dst, half], kv_sem.at[dst, half]
            )
            copy.start()
            loads.append(copy)

    for at, (src, dst) in enumerate(((g_hbm, gs), (q_hbm, qs))):
        for half in range(2):
            for h in range(heads):
                pltpu.make_async_copy(
                    src.at[pl.ds(half * span, span), pl.ds(h * width, width)],
                    dst.at[half, pl.ds(h * span, span), :],
                    load_sem.at[at],
                ).start()
        if at == 0:
            o_copy = pltpu.make_async_copy(o_hbm, o_vm, load_sem.at[2])
            o_copy.start()
    for copy in loads:
        copy.wait()
    first = pos_ref[0] // span
    mark[...] = jnp.full(mark.shape, first, jnp.int32)

    @pl.when(core == 0)
    def _():
        pl.semaphore_wait(barrier, 9)
        signal(gate, mate)

    @pl.when(core == 1)
    def _():
        pl.semaphore_wait(gate, 1)

    def put(src_slot, slot, target):
        return remote(kv.at[src_slot], kv.at[slot], put_sem.at[slot], get_sem.at[slot], target)

    put5 = put(0, FAR, outer_at(1))
    put4 = put(0, 4, inner_at(4))
    put2 = put(0, 2, inner_at(2))
    put1 = put(2 * core, 1, mate)
    put3 = put(2 + 2 * core, 3, mate)
    mark_puts = [
        remote(
            mark,
            marks.at[slot],
            mark_send.at[slot],
            mark_recv.at[slot],
            outer_at(1) if slot == FAR else inner_at(slot),
        )
        for slot in range(1, FAR + 1)
    ]
    for copy in mark_puts[:REACH]:
        copy.start()

    @pl.when(core == 0)
    def _():
        put1.start()

    @pl.when((side == 0) & (core == 0))
    def _():
        put4.start()

    @pl.when(core == 0)
    def _():
        put2.start()

    early = lax.rem(outer, 8) == 0

    def reach_outer():
        @pl.when(core == 1)
        def _():
            pl.semaphore_wait(barrier, 4)
            signal(gate, mate)

        @pl.when(core == 0)
        def _():
            pl.semaphore_wait(gate, 1)

        mark_puts[REACH].start()

        @pl.when(early | (core == 0))
        def _():
            put5.start()

    @pl.when(jnp.logical_not(early))
    def _():
        reach_outer()

    pltpu.make_async_copy(gs, gs, load_sem.at[0]).wait()
    o_copy.wait()
    lane = lax.broadcasted_iota(jnp.int32, (span, width), 1)
    dots = []
    for half in range(2):
        table = jnp.zeros((span, width), F32)
        for h in range(heads):
            g = gs[half, pl.ds(h * span, span), :].astype(F32)
            o = o_vm[pl.ds(half * span, span), pl.ds(h * width, width)].astype(F32)
            table = jnp.where(lane == h, jnp.sum(g * o, axis=1, keepdims=True), table)
        dots.append(table)
    tables = (lse_ref[...] * float(np.log2(np.e)), jnp.concatenate(dots, 0).T)
    for at, table in enumerate(tables):
        for half in range(2):
            pieces = [table[h : h + 1, half * span : (half + 1) * span] for h in range(heads)]
            stats[at, half] = jnp.concatenate(pieces, 1)

    columns = heads * span
    high = jnp.where(first < n_outer * n_inner, 1, 0)
    low = 1 - high

    def unit(slot, key_half, query_half, diagonal):
        k, v = (lax.select(key_half == 1, kv[slot, at, 1], kv[slot, at, 0]) for at in range(2))
        q, g = qs[query_half], gs[query_half]
        probs = jnp.exp2(nt(k, q) * exp_scale - stats[0, query_half])
        if diagonal:
            t = lax.rem(lax.broadcasted_iota(jnp.int32, (1, columns), 1), span)
            u = lax.broadcasted_iota(jnp.int32, (span, 1), 0)
            probs = jnp.where(u <= t, probs, 0.0)
        probs_b = probs.astype(BF16)
        dscores = (probs * (nt(v, g) - stats[1, query_half])).astype(BF16)
        return nn(dscores, q), nn(probs_b, g), nn(k.T, dscores)

    pltpu.make_async_copy(qs, qs, load_sem.at[1]).wait()

    dk, dv, dq = unit(0, low, low, True)
    own[0, 0], own[1, 0], dqt[0] = dk, dv, dq

    @pl.when((side == 0) & (core == 1))
    def _():
        put4.start()

    @pl.when(core == 1)
    def _():
        put2.start()

    @pl.when(jnp.logical_not(early) & (core == 1))
    def _():
        put5.start()

    dk, dv, dq = unit(0, low, high, False)
    own[0, 0] += dk
    own[1, 0] += dv
    dqt[1] = dq

    @pl.when(side == 1)
    def _():
        put4.start()

    def mark_load_of(slot):
        return pltpu.make_async_copy(marks.at[slot], mark_load.at[slot], mark_recv.at[slot])

    def mark_in(slot):
        mark_puts[slot - 1].wait_recv()
        return mark_load_of(slot)

    mark_loads = [mark_in(slot) for slot in range(1, REACH + 1)]
    for copy in mark_loads:
        copy.start()

    far_late = lax.rem(outer, 8) < 2

    @pl.when(jnp.logical_not(far_late))
    def _():
        mark_in(FAR).start()

    dk, dv, dq = unit(0, high, high, True)
    own[0, 1], own[1, 1] = dk, dv
    dqt[1] += dq


    @pl.when(early)
    def _():
        reach_outer()

    for copy in mark_loads:
        copy.wait()

    @pl.when(jnp.logical_not(far_late))
    def _():
        mark_load_of(FAR).wait()

    targets = {1: mate, 2: inner_at(-2), 3: inner_at((1 - core) * (1 - 4 * side) - core), 4: inner_at(-4), FAR: outer_at(-1)}
    term_put = {
        slot: remote(terms.at[slot], came.at[slot], term_send.at[slot], term_recv.at[slot], targets[slot])
        for slot in targets
    }

    def merge(slot, other):
        for at in range(2):
            for half in range(2):
                both = terms[slot, at, half].astype(F32) + came[other, at, half].astype(F32)
                terms[slot, at, half] = both.astype(BF16)

    def packed(*order):
        return sum(slot * 8**at for at, slot in enumerate(order))

    plans = (
        (packed(4, 2, 3, 1, FAR), 0, 9, 2, 9),
        (packed(1, 3, FAR, 4, 2), 2, 1, 4, 3),
        (packed(2, FAR, 1, 4, 3), 0, 9, 2, 9),
        (packed(1, 3, 2, FAR, 4), 2, 4, 3, 9),
        (packed(4, 2, 3, 1, FAR), 0, 9, 4, 9),
        (packed(1, 3, 4, 2, FAR), 2, 1, 4, 3),
        (packed(2, 1, 4, 3, FAR), 0, 9, 4, 9),
        (packed(1, 3, 2, 4, FAR), 1, 3, 4, 9),
        (packed(4, 2, 3, FAR, 1), 0, 9, 2, 9),
        (packed(1, 3, FAR, 4, 2), 2, 1, 4, 3),
        (packed(2, 1, FAR, 4, 3), 0, 9, 2, 9),
        (packed(1, 3, 2, FAR, 4), 2, 4, 3, 9),
    )
    role = 2 * side + core + jnp.where(early, 4, 0) + jnp.where(lax.rem(outer, 8) == 1, 8, 0)

    def planned(column):
        value = jnp.int32(plans[0][column])
        for at in range(1, len(plans)):
            value = jnp.where(role == at, plans[at][column], value)
        return value

    order, pass2_at, pass4_at, merge2_at, merge4_at = (planned(column) for column in range(5))

    def step(at_step, rest):
        slot, rest = lax.rem(rest, 8), rest // 8

        @pl.when((slot == FAR) & far_late)
        def _():
            copy = mark_in(FAR)
            copy.start()
            copy.wait()

        @pl.when(at_step == pass4_at)
        def _():
            put4.wait_recv()
            put3.start()

        @pl.when(at_step == pass2_at)
        def _():
            put2.wait_recv()

        @pl.when((at_step == pass2_at) & (core == 0))
        def _():
            put3.start()

        @pl.when((at_step == pass2_at) & (core == 1))
        def _():
            put1.start()

        @pl.when(jnp.logical_not((slot == 2) | ((slot == 4) & (core == 1))))
        def _():
            put(0, slot, mate).wait_recv()

        there = mark_load[slot, 0, 0]
        there_low = jnp.where(there < n_outer * n_inner, 0, 1)
        run_here = jnp.minimum(first, 2 * n_outer * n_inner - 1 - first)
        run_there = jnp.minimum(there, 2 * n_outer * n_inner - 1 - there)
        earlier = run_there < run_here
        keep = jnp.where(earlier, 1.0, 0.0)
        dk, dv, dq = unit(slot, there_low, high, False)
        key_half = jnp.where(earlier, there_low, 1 - there_low)
        query_half = jnp.where(earlier, low, high)
        dk2, dv2, dq2 = unit(slot, key_half, query_half, False)
        dq_low = dq2 * keep
        dqt[0] += dq_low
        dqt[1] += dq + (dq2 - dq_low)
        for at, (one, two) in enumerate(((dk, dk2), (dv, dv2))):
            two_low = two * keep
            factor = 1.0 if at else scale
            terms[slot, at, 0] = ((one + two_low) * factor).astype(BF16)
            terms[slot, at, 1] = ((two - two_low) * factor).astype(BF16)

        for sent in (1, 3, FAR):

            @pl.when(slot == sent)
            def _():
                term_put[sent].start()

        @pl.when((slot == 4) & ((side == 1) | (core == 0)))
        def _():
            term_put[4].start()

        @pl.when(at_step == merge4_at)
        def _():
            term_put[3].wait_recv()
            merge(4, 3)
            term_put[4].start()

        @pl.when((at_step == merge2_at) & (core == 0))
        def _():
            term_put[3].wait_recv()
            merge(2, 3)
            term_put[2].start()

        @pl.when((at_step == merge2_at) & (core == 1))
        def _():
            term_put[1].wait_recv()
            merge(2, 1)
            term_put[2].start()

        return rest

    lax.fori_loop(0, FAR, step, order)

    in_order = first < n_outer * n_inner
    for half in range(2):
        rank = jnp.where(in_order, half, 1 - half)
        rows = pl.ds(half * span, span)
        dq = (dqt[rank] * scale).T.astype(BF16)
        for h in range(heads):
            out_ref[rows, pl.ds(h * width, width)] = dq[h * span : (h + 1) * span]

    @pl.when(core == 0)
    def _():
        term_put[1].wait_recv()

    @pl.when((core == 1) & (side == 1))
    def _():
        term_put[3].wait_recv()

    direct = jnp.where((core == 0) | (side == 1), 1.0, 0.0)
    for slot in (2, 4, FAR):
        term_put[slot].wait_recv()
    for at in range(2):
        for half in range(2):
            rank = jnp.where(in_order, half, 1 - half)
            total = own[at, rank] * (1.0 if at else scale)
            total += came[1 + 2 * core, at, rank].astype(F32) * direct
            for slot in (2, 4, FAR):
                total += came[slot, at, rank].astype(F32)
            out_ref[pl.ds(half * span, span), pl.ds((heads + at) * width, width)] = total.astype(BF16)

    for copy in mark_puts + [put1, put2, put3, put4, put5] + list(term_put.values()):
        copy.wait_send()


def shards(queries, keys, values, saved_out, saved_lse, out_grad, positions):
    rows, columns = queries.shape
    width = keys.shape[1]
    span = rows // 2
    heads = columns // width
    anywhere = pl.BlockSpec(memory_space=pl.ANY)
    vmem = pl.BlockSpec(memory_space=pltpu.VMEM)
    slots = FAR + 1
    stack = (2, heads * span, width)
    pair = (2, 2, span, width)
    dma = pltpu.SemaphoreType.DMA
    grads = pl.pallas_call(
        functools.partial(kernel, lax.axis_size("outer"), lax.axis_size("inner")),
        out_shape=pltpu.VMEM((rows, columns + 2 * width), BF16),
        in_specs=[anywhere] * 7,
        out_specs=vmem,
        scratch_shapes=[
            pltpu.VMEM(stack, BF16),
            pltpu.VMEM(stack, BF16),
            pltpu.VMEM((2, 2, 1, heads * span), F32),
            pltpu.VMEM((rows, columns), BF16),
            pltpu.VMEM((slots,) + pair, BF16),
            pltpu.VMEM((8, 128), jnp.int32),
            pltpu.VMEM((slots, 8, 128), jnp.int32),
            pltpu.VMEM((2, width, heads * span), F32),
            pltpu.VMEM(pair, F32),
            pltpu.VMEM((slots,) + pair, BF16),
            pltpu.VMEM((slots,) + pair, BF16),
            dma((3,)),
            dma((2, 2)),
            dma((slots,)),
            dma((slots,)),
            pltpu.SMEM((slots, 8, 128), jnp.int32),
            dma((slots,)),
            dma((slots,)),
            dma((slots,)),
            dma((slots,)),
            pltpu.SemaphoreType.REGULAR,
            pltpu.VMEM((heads, rows), F32),
            pltpu.SMEM((rows,), jnp.int32),
            dma((2,)),
        ],
        compiler_params=pltpu.CompilerParams(
            collective_id=0, has_side_effects=True, vmem_limit_bytes=56 * 2**20
        ),
    )(queries, keys, values, saved_out, saved_lse.T, out_grad, positions)
    return grads[:, :columns], grads[:, columns : columns + width], grads[:, columns + width :]


def solution(mesh):
    rows = P(("outer", "inner"), None)
    return jax.shard_map(
        shards,
        mesh=mesh,
        in_specs=(rows,) * 6 + (P(("outer", "inner")),),
        out_specs=(rows,) * 3,
        check_vma=False,
    )
```
